32 devices in a mesh: parts: 2 (over x), sector: 8 (over z, y), term: 2 (over core).
Axes of the slice: x: 2, y: 2, z: 4, core: 2. Of those that a mesh axis runs over, the one named last changes fastest.
Arguments:
- wavefunction: bfloat16 [512, 128, 128], P(('parts', 'sector')), parts along dimension 0, may hold values from -12 to 12
- left_sector: int32 [512], P(('parts', 'sector')), parts along dimension 0, may hold values from 0 to 63, as said below
- right_sector: int32 [512], P(('parts', 'sector')), parts along dimension 0, may hold values from 0 to 63, as said below
- phys_index: int32 [512], P(('parts', 'sector')), parts along dimension 0, may hold values from 0 to 15
- left_environment: bfloat16 [28, 64, 128, 128], P(('parts', 'term'), 'sector'), parts along dimension 0, may hold values from -0.5 to 0.5
- right_environment: bfloat16 [28, 64, 128, 128], P(('parts', 'term'), 'sector'), parts along dimension 0, may hold values from -0.5 to 0.5
- term_weights: bfloat16 [28, 16], P(('parts', 'term')), parts along dimension 0, may hold values from -1.5 to 1.5
Outputs:
- image: float32 [512, 128, 128], P(('parts', 'sector')), parts along dimension 0
- correction: float32 [512, 128, 128], P(('parts', 'sector')), parts along dimension 0
- rayleigh: float32 [2], P('parts'), parts along dimension 0
The draws below stay inside these ranges and needn't reach their ends.
There are 2 independent parts, one for each index of `parts`. The reference program is written for one: setup_inputs(seed, part) draws one part's arguments, and reference() takes and returns one part's arrays. A program takes and returns all parts, laid end to end along the dimension named above; each array names one. Nothing has to cross between parts.
Inputs may be any that keep to these rules, and one draw needn't show every extreme that they name: `left_sector`: for every device of the sector axis, the blocks of one device have at most 8 left sectors lying on it; in every draw one device is named exactly 8 times by the blocks of every device. `right_sector`: block k's right sector lies on device k // 32, among sectors (k // 32) * 8 to (k // 32) * 8 + 7.
All inputs are finite; a program needn't handle non-finite values.
Results may differ from the reference program's by a relative error of at most 0.0048.
Values may be sent and summed in bfloat16 or wider, within the bound.
No kernel may reach another device: no remote copies, remote signals or barrier semaphores. Data moves between devices by JAX's collectives and lax.ppermute only.
A program may use at most 128 MiB of HBM per device.

```python
import jax
import jax.numpy as jnp
from jax import lax

SD = 128
PHYS = 16
TERMS = 14
SEC_DEV = 8
BLK_DEV = 32
NSEC = 64
NBLK = 256
CAP = 8


def draw_wavefunction(key, part):
    key = jax.random.fold_in(key, 13)
    key_values = jax.random.fold_in(key, 0)
    rising = 1.0 + 2.0 * jnp.arange(NBLK, dtype=jnp.float32) / (NBLK - 1)
    values = jax.random.normal(key_values, (NBLK, SD, SD), jnp.float32) * rising[:, None, None]
    return jnp.clip(values, -12.0, 12.0).astype(jnp.bfloat16)


def draw_left_sector(key, part):
    key = jax.random.fold_in(key, 11)
    key_group, key_sources, key_within = jax.random.split(key, 3)
    device_count = NSEC // SEC_DEV
    slots_all = device_count * CAP
    gather_positions = jnp.arange(slots_all, dtype=jnp.int32)
    groups = gather_positions // CAP
    chosen = jax.random.randint(key_group, (), 0, device_count)

    def draw_source(source_key):
        key_scores, key_shuffle = jax.random.split(source_key)
        scores = jax.random.randint(key_scores, (slots_all,), 0, 2 ** 20) * slots_all + gather_positions
        scores = jnp.where(groups == chosen, gather_positions - slots_all, scores)
        ordering = jnp.argsort(scores)
        taken = groups[ordering[:BLK_DEV]]
        shuffle = jax.random.permutation(key_shuffle, BLK_DEV)
        return taken[shuffle]
    targets = jax.vmap(draw_source)(jax.random.split(key_sources, device_count))
    within = jax.random.randint(key_within, (device_count, BLK_DEV), 0, SEC_DEV)
    return (targets * SEC_DEV + within).reshape(-1).astype(jnp.int32)


def draw_right_sector(key, part):
    key = jax.random.fold_in(key, 12)
    device_count = NSEC // SEC_DEV
    within = jax.random.randint(key, (device_count, BLK_DEV), 0, SEC_DEV)
    within = within.at[0, 0].set(0).at[device_count - 1, 0].set(SEC_DEV - 1)
    owners = jnp.arange(device_count, dtype=jnp.int32)[:, None] * SEC_DEV
    return (owners + within).reshape(-1).astype(jnp.int32)


def set_ends(result, key, smallest, largest):
    dims = result.shape
    index_at = [jax.random.randint(jax.random.fold_in(key, axis), (), 0, dims[axis]) for axis in range(len(dims))]
    result = result.at[tuple(index_at)].set(smallest)
    longest = dims.index(max(dims))
    index_at[longest] = (index_at[longest] + 1) % dims[longest]
    return result.at[tuple(index_at)].set(largest)


def block_levels(stream_key, shape, cuts, least, largest):
    gain = 1.0
    for axis_at, blocks in cuts:
        draws = jax.random.uniform(jax.random.fold_in(jax.random.fold_in(stream_key, 6), axis_at), (blocks,), jnp.float32, least / len(cuts), largest / len(cuts))
        gain = gain * jnp.repeat(jnp.exp(draws), shape[axis_at] // blocks).reshape((-1,) + (1,) * (len(shape) - 1 - axis_at))
    return gain


def scatter_about(own_key, extent, scale, bound, cuts=(), held_as=jnp.bfloat16):
    factor_of = block_levels(own_key, extent, cuts, -0.22, 0.18) if cuts else 1.0
    result = jax.random.normal(own_key, extent, jnp.float32) * scale * factor_of
    return jnp.minimum(jnp.maximum(result, -bound), bound).astype(held_as)


def setup_inputs(seed: int = 0, part: int = 0) -> dict:
    key_of = jax.random.split(jax.random.key(seed), 8)
    own_keys = jax.random.split(jax.random.fold_in(key_of[7], part), 8)
    return {
        "wavefunction": draw_wavefunction(jax.random.fold_in(jax.random.fold_in(key_of[7], part), 71), part),
        "left_sector": draw_left_sector(jax.random.fold_in(jax.random.fold_in(key_of[7], part), 71), part),
        "right_sector": draw_right_sector(jax.random.fold_in(jax.random.fold_in(key_of[7], part), 71), part),
        "phys_index": set_ends(jax.random.randint(own_keys[3], (NBLK,), 0, PHYS), jax.random.fold_in(own_keys[3], 1), 0, PHYS - 1).astype(jnp.int32),
        "left_environment": scatter_about(own_keys[4], (TERMS, NSEC, SD, SD), SD ** -0.5, 0.5, ((0, 2), (1, 8))),
        "right_environment": scatter_about(own_keys[5], (TERMS, NSEC, SD, SD), SD ** -0.5, 0.5, ((0, 2), (1, 8))),
        "term_weights": scatter_about(own_keys[6], (TERMS, PHYS), 0.3, 1.5, ((0, 2),)),
    }


def reference(wavefunction, left_sector, right_sector, phys_index, left_environment, right_environment, term_weights):

    def apply_block(inputs):
        lone_sector_term, left_id, right_id, state_id = inputs
        right_environment_block = lax.dynamic_index_in_dim(right_environment, right_id, 1, keepdims=False)
        left_block = lax.dynamic_index_in_dim(left_environment, left_id, 1, keepdims=False)
        weights = lax.dynamic_index_in_dim(term_weights, state_id, 1, keepdims=False).astype(jnp.float32)
        environment_product = jnp.einsum('uv,jyv->juy', lone_sector_term.astype(jnp.float32), right_environment_block.astype(jnp.float32))
        carried = (environment_product * weights[:, None, None]).astype(jnp.bfloat16)
        return jnp.einsum('tij,tjk->ik', left_block.astype(jnp.float32), carried.astype(jnp.float32))
    image = lax.map(apply_block, (wavefunction, left_sector, right_sector, phys_index))
    wave_f32 = wavefunction.astype(jnp.float32)
    norm_wave = jnp.sum(wave_f32 * wave_f32)
    correlation = jnp.sum(wave_f32 * image)
    rayleigh = correlation / norm_wave
    residual = image - rayleigh * wave_f32
    norm_resid = jnp.sum(residual * residual)
    correction = residual * lax.rsqrt(norm_resid / (NBLK * SD * SD) + 1e-06)
    return (image, correction, jnp.reshape(rayleigh, (1,)))
```

```python
import functools

import jax
import jax.numpy as jnp
from jax import lax
from jax.experimental import pallas as pl
from jax.experimental.pallas import tpu as pltpu
from jax.sharding import PartitionSpec as P

BOTH = ("sector", "term")
VMEM_LIMIT = 48 * 2**20


def on_device_any(
    wavefunction,
    left_sector,
    right_sector,
    phys_index,
    left_environment,
    right_environment,
    term_weights,
):
    blocks = wavefunction.shape[0]
    sector_dim = wavefunction.shape[1]
    sector_count = lax.axis_size("sector")
    per_device = right_environment.shape[1]
    capacity = 2 * max(1, blocks // sector_count)
    own_index = lax.axis_index("sector")
    right_local = right_sector - own_index * per_device
    target = left_sector // per_device
    positions = jnp.arange(blocks)
    earlier = (target[None, :] == target[:, None]) & (positions[None, :] < positions[:, None])
    placement_order = jnp.sum(earlier.astype(jnp.int32), axis=1)
    physical_selector_matrix = (
        phys_index[:, None] == jnp.arange(term_weights.shape[1])[None, :]
    ).astype(jnp.bfloat16)
    slot_index = target * capacity + placement_order
    slot_count = sector_count * capacity
    selector_f = (jnp.arange(slot_count)[:, None] == slot_index[None, :]).astype(jnp.float32)
    wanted = jnp.dot(
        selector_f, (left_sector % per_device).astype(jnp.float32), precision=lax.Precision.HIGHEST
    ).astype(jnp.int32)
    requests = lax.all_to_all(
        wanted.reshape(sector_count, capacity), "sector", split_axis=0, concat_axis=0, tiled=True
    )
    picked = jnp.take(left_environment, requests.reshape(-1), axis=1)
    picked = jnp.moveaxis(picked, 0, 1).reshape(
        sector_count, capacity, left_environment.shape[0], sector_dim, sector_dim
    )
    fetched = lax.all_to_all(picked, "sector", split_axis=0, concat_axis=0, tiled=True)
    left_blocks = jnp.take(
        fetched.reshape(slot_count, left_environment.shape[0], sector_dim, sector_dim),
        slot_index,
        axis=0,
    )
    right_taken = jnp.take(right_environment, right_local, axis=1)
    block_weights = jnp.dot(
        physical_selector_matrix, term_weights.T, preferred_element_type=jnp.float32
    )
    environment_product = jnp.einsum(
        "kab,tkcb->ktac", wavefunction, right_taken, preferred_element_type=jnp.float32
    )
    carried = (environment_product * block_weights[:, :, None, None]).astype(jnp.bfloat16)
    image_partial_result = jnp.einsum(
        "ktij,ktjc->kic", left_blocks, carried, preferred_element_type=jnp.float32
    )
    image = lax.psum(image_partial_result, "term")
    wave_f32 = wavefunction.astype(jnp.float32)
    norm_wave = jnp.sum(wave_f32 * wave_f32)
    correlation = jnp.sum(wave_f32 * image)
    entries = blocks * sector_count * sector_dim * sector_dim
    norm_all, correlation_all = lax.psum((norm_wave, correlation), "sector")
    rayleigh = correlation_all / norm_all
    residual = image - rayleigh * wave_f32
    norm_resid = lax.psum(jnp.sum(residual * residual), "sector")
    correction = residual * lax.rsqrt(norm_resid / entries + 1e-06)
    return (image, correction, jnp.reshape(rayleigh, (1,)))


def pairs_of(target, chosen=lambda z, y, c: True):
    found = []
    for z in range(4):
        for y in range(2):
            for c in range(2):
                if chosen(z, y, c):
                    to = target(z, y, c)
                    if 0 <= to[0] < 4:
                        found.append(((z * 2 + y) * 2 + c, (to[0] * 2 + to[1]) * 2 + to[2]))
    return found


def inner(z, y, c):
    return z in (1, 2)


def outer(z, y, c):
    return z in (0, 3)


DIAGONAL = pairs_of(lambda z, y, c: (z, 1 - y, 1 - c), lambda z, y, c: y != c)
CORE = pairs_of(lambda z, y, c: (z, y, 1 - c))
CORE_INNER = pairs_of(lambda z, y, c: (z, y, 1 - c), inner)
COLUMN = pairs_of(lambda z, y, c: (z, 1 - y, c))
COLUMN_INNER = pairs_of(lambda z, y, c: (z, 1 - y, c), inner)
UP = pairs_of(lambda z, y, c: (z + 1, y, c))
DOWN = pairs_of(lambda z, y, c: (z - 1, y, c))
UP_INNER = pairs_of(lambda z, y, c: (z + 1, y, c), inner)
DOWN_INNER = pairs_of(lambda z, y, c: (z - 1, y, c), inner)
GUEST = pairs_of(lambda z, y, c: (1 if z == 0 else 2, y, c), outer)
GUEST_BACK = pairs_of(lambda z, y, c: (0 if z == 1 else 3, y, c), inner)
NEAR = pairs_of(lambda z, y, c: (z ^ 1, y, c))
FAR = pairs_of(lambda z, y, c: (z ^ 2, y, c))


def move(array, pairs):
    return lax.ppermute(array, BOTH, pairs)


def carried_of(wave, right, weights):
    terms, dim, _ = right.shape
    product = lax.dot_general(
        wave,
        right.reshape(terms * dim, dim),
        (((1,), (1,)), ((), ())),
        preferred_element_type=jnp.float32,
    )
    return (product * weights).astype(jnp.bfloat16)


def applied(left, carried):
    terms, dim, _ = left.shape
    lefts = jnp.concatenate([left[t] for t in range(terms)], axis=1)
    stacked = jnp.concatenate(
        [carried[:, t * dim : (t + 1) * dim] for t in range(terms)], axis=0
    )
    return jnp.dot(lefts, stacked, preferred_element_type=jnp.float32)


def near_kernel(
    table, weights, wave_own, wave_other, right_mine, right_sib, left_mine, left_below, left_above,
    own_out, other_out, wave, right, left, sems,
):
    blocks = own_out.shape[0]
    copies = [
        pltpu.make_async_copy(source, target, sems.at[n])
        for n, (source, target) in enumerate(
            (
                (wave_own, wave.at[0]),
                (wave_other, wave.at[1]),
                (right_mine, right.at[0]),
                (right_sib, right.at[1]),
                (left_mine, left.at[0]),
                (left_below, left.at[1]),
                (left_above, left.at[2]),
            )
        )
    ]
    for copy in copies:
        copy.start()
    own_out[...] = jnp.zeros_like(own_out)
    other_out[...] = jnp.zeros_like(other_out)
    for copy in copies:
        copy.wait()
    for relation in range(2):

        @pl.loop(0, blocks)
        def _(slot):
            row = relation * blocks + slot
            stage = table[row, 0]

            @pl.when((stage >= 0) & (stage < 3))
            def _():
                block_right = right[table[row, 3], :, table[row, 4]]
                carried = carried_of(
                    wave[relation, table[row, 1]], block_right, weights[pl.ds(row, 1), :]
                )
                result = applied(left[stage, :, table[row, 2]], carried)
                if relation == 0:
                    own_out[slot] = result
                else:
                    other_out[slot] = result.astype(jnp.bfloat16)


def carry_kernel(
    table, weights, wave_own, wave_other, wave_guest, right_mine, right_sib, guest_mine, guest_sib,
    out, wave, guest, right, sems,
):
    slots = guest.shape[0]
    copies = [
        pltpu.make_async_copy(source, target, sems.at[n])
        for n, (source, target) in enumerate(
            (
                (wave_own, wave.at[0]),
                (wave_other, wave.at[1]),
                (wave_guest, guest),
                (right_mine, right.at[0]),
                (right_sib, right.at[1]),
                (guest_mine, right.at[2]),
                (guest_sib, right.at[3]),
            )
        )
    ]
    for copy in copies:
        copy.start()
    for copy in copies:
        copy.wait()

    @pl.loop(0, slots)
    def _(row):
        @pl.when(table[row, 0] == 3)
        def _():
            block_right = right[table[row, 3], :, table[row, 4]]
            relation = row // (slots // 2)
            out[row] = carried_of(
                wave[relation, table[row, 1]], block_right, weights[pl.ds(row, 1), :]
            )

    @pl.loop(slots, 2 * slots)
    def _(row):
        @pl.when(table[row, 0] == 3)
        def _():
            block_right = right[2 + table[row, 3], :, table[row, 4]]
            out[row] = carried_of(guest[row - slots], block_right, weights[pl.ds(row, 1), :])


def far_kernel(
    table, low, carried, left_two_below, left_two_above, own, other,
    own_out, other_out, guest_own_out, guest_other_out, held, left, sems, left_sem,
):
    half = own_out.shape[0]
    rows = 4 * half

    @pl.when(low[0] == 1)
    def _():
        pltpu.make_async_copy(left_two_above, left, left_sem.at[0]).start()

    @pl.when(low[0] == 0)
    def _():
        pltpu.make_async_copy(left_two_below, left, left_sem.at[0]).start()

    for row in range(rows):

        @pl.when(table[row, 0] == 3)
        def _():
            pltpu.make_async_copy(carried.at[row], held.at[row], sems.at[row]).start()

    own_out[...] = own[...]
    other_out[...] = other[...]
    guest_own_out[...] = jnp.zeros_like(guest_own_out)
    guest_other_out[...] = jnp.zeros_like(guest_other_out)
    pltpu.make_async_copy(left_two_above, left, left_sem.at[0]).wait()
    for part, target in ((2, guest_own_out), (3, guest_other_out), (0, own_out), (1, other_out)):

        @pl.loop(0, half)
        def _(slot):
            row = part * half + slot

            @pl.when(table[row, 0] == 3)
            def _():
                pltpu.make_async_copy(carried.at[row], held.at[row], sems.at[row]).wait()
                result = applied(left[:, table[row, 2]], held[row])
                target[slot] = result.astype(target.dtype)


def pick_kernel(table, first, second, out):
    slots = out.shape[0]
    half = slots // 2

    @pl.loop(0, half)
    def _(slot):
        out[slot] = first[table[slot, 1]]
        out[half + slot] = second[table[half + slot, 1]]


def gather_kernel(
    table, first_own, last_own, guest_own, first_sib, last_sib, guest_sib, wave, image, sums
):
    blocks = image.shape[0]
    zero = jnp.zeros((8, 128), jnp.float32)

    def folded(value):
        return jnp.sum(value.reshape(-1, 8, 128), axis=0)

    def place(k, totals):
        for code, source in enumerate(
            (first_own, last_own, guest_own, first_sib, last_sib, guest_sib)
        ):

            @pl.when(table[k, 0] == code)
            def _():
                image[k] = source[table[k, 1]].astype(jnp.float32)

        value = wave[k].astype(jnp.float32)
        return totals[0] + folded(value * value), totals[1] + folded(value * image[k])

    norm_map, correlation_map = lax.fori_loop(0, blocks, place, (zero, zero))
    norm = jnp.sum(norm_map, keepdims=True)
    correlation = jnp.sum(correlation_map, keepdims=True)
    ratio = jnp.where(norm > 0, correlation / jnp.where(norm > 0, norm, 1.0), 0.0)

    def rest(k, total):
        residual = image[k] - ratio * wave[k].astype(jnp.float32)
        return total + folded(residual * residual)

    resid = jnp.sum(lax.fori_loop(0, blocks, rest, zero), keepdims=True)
    line = lax.broadcasted_iota(jnp.int32, (8, 128), 0)
    sums[...] = jnp.where(
        line == 0, norm, jnp.where(line == 1, correlation, jnp.where(line == 2, resid, 0.0))
    )


def ratio_of(norm, correlation):
    return jnp.where(norm > 0, correlation / jnp.where(norm > 0, norm, 1.0), 0.0)


def merged(one, two):
    low, high = jnp.minimum(one[0], two[0]), jnp.maximum(one[0], two[0])
    norm = one[0] + two[0]
    gap = ratio_of(one[0], one[1]) - ratio_of(two[0], two[1])
    shared = low * jnp.where(norm > 0, high / jnp.where(norm > 0, norm, 1.0), 0.0)
    return jnp.stack([norm, one[1] + two[1], one[2] + two[2] + gap * gap * shared])


def ranks(key):
    at = jnp.arange(key.shape[-1])
    mine, others = key[..., :, None], key[..., None, :]
    before = (others < mine) | ((others == mine) & (at[None, :] < at[:, None]))
    return jnp.sum(before.astype(jnp.int32), axis=-1)


def call(kernel, out_shape, in_spaces, out_spaces, scratch, flops, bytes_accessed):
    return pl.pallas_call(
        kernel,
        out_shape=out_shape,
        in_specs=[pl.BlockSpec(memory_space=space) for space in in_spaces],
        out_specs=jax.tree.map(lambda space: pl.BlockSpec(memory_space=space), out_spaces),
        scratch_shapes=scratch,
        compiler_params=pltpu.CompilerParams(vmem_limit_bytes=VMEM_LIMIT),
        cost_estimate=pl.CostEstimate(
            flops=flops, bytes_accessed=bytes_accessed, transcendentals=0
        ),
    )


def on_device(
    wavefunction,
    left_sector,
    right_sector,
    phys_index,
    left_environment,
    right_environment,
    term_weights,
):
    blocks, dim, _ = wavefunction.shape
    terms, per_device = left_environment.shape[:2]
    most = 2 * max(1, blocks // 8)
    first_slots = blocks - most
    index = lax.axis_index("sector")
    z, y, c = index // 2, index % 2, lax.axis_index("term")
    straight = y == c

    def mine_of(own, swapped):
        return jnp.where(straight, own, swapped)

    left_swapped = move(left_environment, DIAGONAL)
    left_mine = mine_of(left_environment, left_swapped)
    left_below = move(left_mine, UP)
    left_above = move(left_mine, DOWN)
    right_held, _ = lax.optimization_barrier((right_environment, left_swapped))
    right_mine = mine_of(right_environment, move(right_held, DIAGONAL))
    left_two_below = move(left_below, UP_INNER)
    left_two_above = move(left_above, DOWN_INNER)

    info = jnp.stack([left_sector, right_sector - index * per_device, phys_index])
    info_other = move(info, COLUMN)
    half = blocks // 2
    wave_half = lax.dynamic_slice_in_dim(wavefunction, c * half, half, 0)
    wave_half = move(wave_half, COLUMN)
    wave_sib = move(wave_half, CORE)
    wave_other = jnp.concatenate(
        [jnp.where(c == 0, wave_half, wave_sib), jnp.where(c == 0, wave_sib, wave_half)]
    )
    weights_sib = move(term_weights, CORE)
    weights_mine = mine_of(term_weights, weights_sib)
    right_sib = move(right_mine, CORE)

    infos = jnp.stack([info, info_other, info])
    left_device = infos[:, 0] // per_device
    parity = jnp.stack([c, c, 1 - c])[:, None]
    step = left_device // 2 - z
    stage = jnp.where(
        step == 0, 0, jnp.where(step == -1, 1, jnp.where(step == 1, 2, 3))
    )
    here = left_device % 2 == parity
    guest = here & (jnp.abs(step) == 3)
    stage = jnp.where(here & ~guest, stage, -1)
    key = jnp.where(stage < 0, 0, jnp.where(stage == 3, 2, 1))
    place = ranks(key)
    guest_place = ranks(jnp.where(guest, 0, 1))
    side = jnp.where(jnp.arange(2) == 0, y, 1 - y)
    right_from = jnp.broadcast_to((side != c).astype(jnp.int32)[:, None], (2, blocks))
    at = jnp.broadcast_to(jnp.arange(blocks)[None], (2, blocks))
    fields = jnp.stack(
        [stage[:2], at, infos[:2, 0] % per_device, right_from, infos[:2, 1], infos[:2, 2]], axis=-1
    )

    def ordered(places, count, values):
        chosen = (jnp.arange(count)[None, :, None] == places[:, None, :]).astype(jnp.float32)
        return jnp.einsum(
            "rsk,rkf->rsf", chosen, values.astype(jnp.float32), precision=lax.Precision.HIGHEST
        ).astype(jnp.int32)

    table = ordered(place[:2], blocks, fields)
    guest_fields = jnp.concatenate(
        [jnp.where(guest[:2], 3, -1)[:, :, None], fields[:, :, 1:]], axis=-1
    )
    guest_table = ordered(guest_place[:2], most, guest_fields).reshape(2 * most, -1)
    far_table = table[:, first_slots:].reshape(2 * most, -1)
    table = table.reshape(2 * blocks, -1)

    def weight_rows(tab):
        state = (tab[:, 5][:, None] == jnp.arange(term_weights.shape[1])[None, :]).astype(
            jnp.bfloat16
        )
        rows = jnp.dot(state, weights_mine.T, preferred_element_type=jnp.float32)
        return jnp.broadcast_to(rows[:, :, None], rows.shape + (dim,)).reshape(-1, terms * dim)

    ANY, VMEM, SMEM = pl.ANY, pltpu.VMEM, pltpu.SMEM
    bf16, f32 = jnp.bfloat16, jnp.float32
    square = (dim, dim)
    env = (terms, per_device) + square
    wave_guest = call(
        pick_kernel,
        jax.ShapeDtypeStruct((2 * most,) + square, bf16),
        [SMEM, VMEM, VMEM],
        VMEM,
        [],
        0,
        4 * 2**20,
    )(guest_table, wavefunction, wave_other)
    is_outer = (z == 0) | (z == 3)
    guest_table = jnp.where(is_outer, guest_table, -1)
    wave_guest = move(wave_guest, GUEST)
    guest_got = move(guest_table, GUEST)
    right_guest = move(right_mine, GUEST)
    right_guest_sib = move(right_guest, CORE_INNER)
    late_table = jnp.concatenate([far_table, jnp.where(is_outer, -1, guest_got)])

    own, other = call(
        near_kernel,
        (
            jax.ShapeDtypeStruct((blocks,) + square, f32),
            jax.ShapeDtypeStruct((blocks,) + square, bf16),
        ),
        [SMEM, VMEM] + [ANY] * 7,
        (VMEM, VMEM),
        [
            pltpu.VMEM((2, blocks) + square, bf16),
            pltpu.VMEM((2,) + env, bf16),
            pltpu.VMEM((3,) + env, bf16),
            pltpu.SemaphoreType.DMA((7,)),
        ],
        4 * 24 * terms * dim**3,
        14 * 2**20,
    )(
        table, weight_rows(table), wavefunction, wave_other, right_mine, right_sib,
        left_mine, left_below, left_above,
    )
    first_got = move(other[:first_slots], COLUMN)
    first_own = own[:first_slots] + first_got.astype(f32)
    first_sib = move(first_own, CORE)

    carried = call(
        carry_kernel,
        jax.ShapeDtypeStruct((4 * most, dim, terms * dim), bf16),
        [SMEM, VMEM] + [ANY] * 7,
        VMEM,
        [
            pltpu.VMEM((2, blocks) + square, bf16),
            pltpu.VMEM((2 * most,) + square, bf16),
            pltpu.VMEM((4,) + env, bf16),
            pltpu.SemaphoreType.DMA((7,)),
        ],
        2 * 16 * terms * dim**3,
        18 * 2**20,
    )(
        late_table, weight_rows(late_table), wavefunction, wave_other, wave_guest,
        right_mine, right_sib, right_guest, right_guest_sib,
    )
    low = (z < 2).astype(jnp.int32).reshape(1)
    last = jax.ShapeDtypeStruct((most,) + square, f32)
    last_sent = jax.ShapeDtypeStruct((most,) + square, bf16)
    last_own, last_other, guest_own, guest_other = call(
        far_kernel,
        (last, last_sent, last, last_sent),
        [SMEM, SMEM] + [ANY] * 3 + [VMEM] * 2,
        (VMEM,) * 4,
        [
            pltpu.VMEM((4 * most, dim, terms * dim), bf16),
            pltpu.VMEM(env, bf16),
            pltpu.SemaphoreType.DMA((4 * most,)),
            pltpu.SemaphoreType.DMA((1,)),
        ],
        2 * 16 * terms * dim**3,
        8 * 2**20,
    )(
        late_table, low, carried, left_two_below, left_two_above,
        own[first_slots:], other[first_slots:],
    )
    guest_full = guest_own + move(guest_other, COLUMN_INNER).astype(f32)
    guest_home = move(guest_full.astype(bf16), GUEST_BACK)
    last_full = last_own + move(last_other, COLUMN).astype(f32)
    last_sib = move(last_full, CORE)
    guest_sib = move(guest_home, CORE)

    home = stage[0::2], place[0::2], guest[0::2], guest_place[0::2], here[0::2]

    def source_of(which):
        _, placed, is_guest, guest_at, _ = (value[which] for value in home)
        code = jnp.where(is_guest, 2, jnp.where(placed < first_slots, 0, 1))
        slot = jnp.where(is_guest, guest_at, jnp.where(placed < first_slots, placed, placed - first_slots))
        return jnp.stack([code + 3 * which, slot], axis=-1)

    sources = jnp.where(home[4][0][:, None], source_of(0), source_of(1))
    image, sums = call(
        gather_kernel,
        (
            jax.ShapeDtypeStruct((blocks,) + square, f32),
            jax.ShapeDtypeStruct((8, 128), f32),
        ),
        [SMEM] + [VMEM] * 7,
        (VMEM, VMEM),
        [],
        blocks * 8 * dim * dim,
        8 * 2**20,
    )(sources, first_own, last_full, guest_home, first_sib, last_sib, guest_sib, wavefunction)
    totals = sums[:3]
    for pairs in (COLUMN, NEAR, FAR):
        totals = merged(totals, move(totals, pairs))
    rayleigh = totals[1, :1] / totals[0, :1]
    entries = blocks * 8 * dim * dim
    scale = lax.rsqrt(totals[2, :1] / entries + 1e-06)
    residual = image - rayleigh[:, None, None] * wavefunction.astype(f32)
    return image, residual * scale[:, None, None], rayleigh


def solution(mesh):
    placed = (
        P(("parts", "sector"), None, None),
        P(("parts", "sector")),
        P(("parts", "sector")),
        P(("parts", "sector")),
        P(("parts", "term"), "sector", None, None),
        P(("parts", "term"), "sector", None, None),
        P(("parts", "term"), None),
    )
    paired = mesh.shape["sector"] == 8 and mesh.shape["term"] == 2
    return jax.shard_map(
        on_device if paired else on_device_any,
        mesh=mesh,
        in_specs=placed,
        out_specs=(
            P(("parts", "sector"), None, None),
            P(("parts", "sector"), None, None),
            P("parts"),
        ),
        check_vma=False,
    )
```

```python
import functools

import jax
import jax.numpy as jnp
from jax import lax
from jax.experimental import pallas as pl
from jax.experimental.pallas import tpu as pltpu
from jax.sharding import PartitionSpec as P

BOTH = ("sector", "term")
VMEM_LIMIT = 48 * 2**20


def on_device_any(
    wavefunction,
    left_sector,
    right_sector,
    phys_index,
    left_environment,
    right_environment,
    term_weights,
):
    blocks = wavefunction.shape[0]
    sector_dim = wavefunction.shape[1]
    sector_count = lax.axis_size("sector")
    per_device = right_environment.shape[1]
    capacity = 2 * max(1, blocks // sector_count)
    own_index = lax.axis_index("sector")
    right_local = right_sector - own_index * per_device
    target = left_sector // per_device
    positions = jnp.arange(blocks)
    earlier = (target[None, :] == target[:, None]) & (positions[None, :] < positions[:, None])
    placement_order = jnp.sum(earlier.astype(jnp.int32), axis=1)
    physical_selector_matrix = (
        phys_index[:, None] == jnp.arange(term_weights.shape[1])[None, :]
    ).astype(jnp.bfloat16)
    slot_index = target * capacity + placement_order
    slot_count = sector_count * capacity
    selector_f = (jnp.arange(slot_count)[:, None] == slot_index[None, :]).astype(jnp.float32)
    wanted = jnp.dot(
        selector_f, (left_sector % per_device).astype(jnp.float32), precision=lax.Precision.HIGHEST
    ).astype(jnp.int32)
    requests = lax.all_to_all(
        wanted.reshape(sector_count, capacity), "sector", split_axis=0, concat_axis=0, tiled=True
    )
    picked = jnp.take(left_environment, requests.reshape(-1), axis=1)
    picked = jnp.moveaxis(picked, 0, 1).reshape(
        sector_count, capacity, left_environment.shape[0], sector_dim, sector_dim
    )
    fetched = lax.all_to_all(picked, "sector", split_axis=0, concat_axis=0, tiled=True)
    left_blocks = jnp.take(
        fetched.reshape(slot_count, left_environment.shape[0], sector_dim, sector_dim),
        slot_index,
        axis=0,
    )
    right_taken = jnp.take(right_environment, right_local, axis=1)
    block_weights = jnp.dot(
        physical_selector_matrix, term_weights.T, preferred_element_type=jnp.float32
    )
    environment_product = jnp.einsum(
        "kab,tkcb->ktac", wavefunction, right_taken, preferred_element_type=jnp.float32
    )
    carried = (environment_product * block_weights[:, :, None, None]).astype(jnp.bfloat16)
    image_partial_result = jnp.einsum(
        "ktij,ktjc->kic", left_blocks, carried, preferred_element_type=jnp.float32
    )
    image = lax.psum(image_partial_result, "term")
    wave_f32 = wavefunction.astype(jnp.float32)
    norm_wave = jnp.sum(wave_f32 * wave_f32)
    correlation = jnp.sum(wave_f32 * image)
    entries = blocks * sector_count * sector_dim * sector_dim
    norm_all, correlation_all = lax.psum((norm_wave, correlation), "sector")
    rayleigh = correlation_all / norm_all
    residual = image - rayleigh * wave_f32
    norm_resid = lax.psum(jnp.sum(residual * residual), "sector")
    correction = residual * lax.rsqrt(norm_resid / entries + 1e-06)
    return (image, correction, jnp.reshape(rayleigh, (1,)))


def pairs_of(target, chosen=lambda z, y, c: True):
    found = []
    for z in range(4):
        for y in range(2):
            for c in range(2):
                if chosen(z, y, c):
                    to = target(z, y, c)
                    if 0 <= to[0] < 4:
                        found.append(((z * 2 + y) * 2 + c, (to[0] * 2 + to[1]) * 2 + to[2]))
    return found


def inner(z, y, c):
    return z in (1, 2)


def outer(z, y, c):
    return z in (0, 3)


def straight(z, y, c):
    return y == c


def crossed(z, y, c):
    return y != c


def both(one, two):
    return lambda z, y, c: one(z, y, c) and two(z, y, c)


def up(z, y, c):
    return z + 1, y, c


def down(z, y, c):
    return z - 1, y, c


def other_core(z, y, c):
    return z, y, 1 - c


def other_column(z, y, c):
    return z, 1 - y, c


def inward(z, y, c):
    return (1 if z == 0 else 2), y, c


def outward(z, y, c):
    return (0 if z == 1 else 3), y, c


def outward_crossed(z, y, c):
    return (0 if z == 1 else 3), 1 - y, c


DIAGONAL = pairs_of(lambda z, y, c: (z, 1 - y, 1 - c), crossed)
CORE = pairs_of(other_core)
COLUMN = pairs_of(other_column)
COLUMN_INNER = pairs_of(other_column, inner)
GUEST = pairs_of(inward, outer)
GUEST_BACK = pairs_of(outward, inner)
GUEST_BACK_CROSSED = pairs_of(outward_crossed, inner)


def move(array, pairs):
    return lax.ppermute(array, BOTH, pairs)


def carried_of(wave, right, weights):
    terms, dim, _ = right.shape
    product = lax.dot_general(
        wave,
        right.reshape(terms * dim, dim),
        (((1,), (1,)), ((), ())),
        preferred_element_type=jnp.float32,
    )
    return (product * weights).astype(jnp.bfloat16)


def applied(left, carried):
    terms, dim, _ = left.shape
    lefts = jnp.concatenate([left[t] for t in range(terms)], axis=1)
    stacked = jnp.concatenate(
        [carried[:, t * dim : (t + 1) * dim] for t in range(terms)], axis=0
    )
    return jnp.dot(lefts, stacked, preferred_element_type=jnp.float32)


def choose(flag, one, two, target, sem):
    @pl.when(flag)
    def _():
        pltpu.make_async_copy(one, target, sem).start()

    @pl.when(jnp.logical_not(flag))
    def _():
        pltpu.make_async_copy(two, target, sem).start()


def grouped(low, high, step, body):
    @pl.loop(0, (high - low + step - 1) // step)
    def _(group):
        for n in range(step):
            body(jnp.minimum(low + group * step + n, high - 1))


def count_of(table, base, rows, stage):
    def add(row, total):
        return total + (table[base + row, 0] == stage).astype(jnp.int32)

    return lax.fori_loop(0, rows, add, jnp.int32(0))


def near_kernel(
    table, weights, wave_in, right_mine, right_sib, left_mine, below, above,
    first, last, carried_out,
    result, carried, wave, right, left, sems, carried_sems,
):
    blocks = wave.shape[0]
    most = last.shape[0]
    first_slots = blocks - most
    copies = [
        pltpu.make_async_copy(source, target, sems.at[n])
        for n, (source, target) in enumerate(
            (
                (wave_in, wave),
                (right_mine, right.at[0]),
                (right_sib, right.at[1]),
                (left_mine, left.at[0]),
                (below, left.at[1]),
                (above, left.at[2]),
            )
        )
    ]
    for copy in copies:
        copy.start()
    result[...] = jnp.zeros_like(result)
    skipped = count_of(table, 0, blocks, -1)
    end = blocks - count_of(table, 0, blocks, 3)
    for copy in copies[:3]:
        copy.wait()

    def carry(slot):
        return carried_of(
            wave[table[slot, 1]], right[table[slot, 3], :, table[slot, 4]], weights[pl.ds(table[slot, 5], 1), :]
        )

    def written(slot):
        at = slot - first_slots
        return pltpu.make_async_copy(carried.at[at], carried_out.at[at], carried_sems.at[at])

    def keep(slot):
        carried[slot - first_slots] = carry(slot)

    grouped(end, blocks, 4, keep)

    @pl.loop(end, blocks)
    def _(slot):
        written(slot).start()

    for copy in copies[3:]:
        copy.wait()

    def apply(slot):
        found = applied(left[table[slot, 0], :, table[slot, 2]], carry(slot))
        result[slot] = found.astype(result.dtype)

    grouped(skipped, end, 4, apply)
    out = pltpu.make_async_copy(result.at[pl.ds(0, first_slots)], first, sems.at[len(copies)])
    out.start()
    last[...] = result[first_slots:]
    out.wait()

    @pl.loop(end, blocks)
    def _(slot):
        written(slot).wait()


def sum_kernel(one, two, out):
    out[...] = one[...].astype(out.dtype) + two[...].astype(out.dtype)


def far_kernel(
    flags, table, guest_table, weights, carried_own, carried_other, below, above, own, other,
    wave_own, wave_other, right_mine, right_sib,
    own_out, other_out, guest_own_out, guest_other_out,
    held, held_guest, wave, right, left, sems, guest_sems, wave_sems, left_sem,
):
    rows = held.shape[0]
    half = rows // 2
    for relation, source in enumerate((wave_own, wave_other)):
        pltpu.make_async_copy(
            source.at[pl.ds(0, half)], wave.at[pl.ds(relation * half, half)], wave_sems.at[relation]
        ).start()

    @pl.loop(0, rows)
    def _(row):
        @pl.when(guest_table[row, 0] == 3)
        def _():
            sector = guest_table[row, 4]
            choose(
                flags[1 + row // half] == 0, right_mine.at[:, sector], right_sib.at[:, sector],
                right.at[row], guest_sems.at[row],
            )

    choose(flags[0] == 1, above, below, left, left_sem.at[0])

    @pl.loop(0, half)
    def _(slot):
        for part, carried in enumerate((carried_own, carried_other)):
            row = part * half + slot

            @pl.when(table[row, 0] == 3)
            def _():
                pltpu.make_async_copy(carried.at[slot], held.at[row], sems.at[row]).start()

    own_out[...] = own[...]
    other_out[...] = other[...]
    guest_own_out[...] = jnp.zeros_like(guest_own_out)
    guest_other_out[...] = jnp.zeros_like(guest_other_out)
    for relation, source in enumerate((wave_own, wave_other)):
        pltpu.make_async_copy(
            source.at[pl.ds(0, half)], wave.at[pl.ds(relation * half, half)], wave_sems.at[relation]
        ).wait()

    @pl.loop(0, rows)
    def _(row):
        @pl.when(guest_table[row, 0] == 3)
        def _():
            pltpu.make_async_copy(right_mine.at[:, 0], right.at[row], guest_sems.at[row]).wait()

    def carry(row):
        held_guest[row] = carried_of(
            wave[row], right[row], weights[pl.ds(guest_table[row, 5], 1), :]
        )

    counts = [count_of(guest_table, part * half, half, 3) for part in range(2)]
    for part in range(2):
        grouped(part * half, part * half + counts[part], 4, carry)
    pltpu.make_async_copy(above, left, left_sem.at[0]).wait()
    for part, target in enumerate((guest_own_out, guest_other_out)):

        def apply_guest(row):
            result = applied(left[:, guest_table[row, 2]], held_guest[row])
            target[row - part * half] = result.astype(target.dtype)

        grouped(part * half, part * half + counts[part], 4, apply_guest)

    @pl.loop(0, rows)
    def _(row):
        @pl.when(table[row, 0] == 3)
        def _():
            pltpu.make_async_copy(carried_own.at[0], held.at[row], sems.at[row]).wait()

    for part, target in enumerate((own_out, other_out)):

        def apply_own(row):
            result = applied(left[:, table[row, 2]], held[row])
            target[row - part * half] = result.astype(target.dtype)

        high = (part + 1) * half
        grouped(high - count_of(table, part * half, half, 3), high, 4, apply_own)


def pick_kernel(table, own, facts, out):
    slots = out.shape[0] - 1
    out[slots] = facts[0]

    @pl.loop(0, slots)
    def _(slot):
        out[slot] = own[table[slot, 1]]


def folded(value):
    return jnp.sum(value.reshape(-1, 8, 128), axis=0)


def first_kernel(table, first_own, first_sib, wave, image, sums):
    blocks = image.shape[0]
    zero = jnp.zeros((8, 128), jnp.float32)
    image[...] = jnp.zeros_like(image)

    def place(k, totals):
        for code, source in ((0, first_own), (3, first_sib)):

            @pl.when(table[k, 0] == code)
            def _():
                image[k] = source[table[k, 1]]

        kept = ((table[k, 0] == 0) | (table[k, 0] == 3)).astype(jnp.float32)
        value = wave[k].astype(jnp.float32) * kept
        return totals[0] + folded(value * value), totals[1] + folded(value * image[k])

    norm_map, correlation_map = lax.fori_loop(0, blocks, place, (zero, zero), unroll=2)
    norm = jnp.sum(norm_map, keepdims=True)
    correlation = jnp.sum(correlation_map, keepdims=True)
    ratio = ratio_of(norm, correlation)

    def rest(k, total):
        kept = ((table[k, 0] == 0) | (table[k, 0] == 3)).astype(jnp.float32)
        residual = image[k] - ratio * (wave[k].astype(jnp.float32) * kept)
        return total + folded(residual * residual)

    resid = jnp.sum(lax.fori_loop(0, blocks, rest, zero, unroll=2), keepdims=True)
    sums[...] = lined(norm, correlation, resid)


def lined(*values):
    line = lax.broadcasted_iota(jnp.int32, (8, 128), 0)
    result = jnp.zeros((8, 128), jnp.float32)
    for n, value in enumerate(values):
        result = jnp.where(line == n, value, result)
    return result


def last_kernel(
    table, sums_first, last_own, guest_own, last_sib, guest_sib, wave, held,
    image, sums, late, out_sems,
):
    blocks = wave.shape[0]
    most = last_own.shape[0]
    zero = jnp.zeros((8, 128), jnp.float32)
    for n, source in enumerate((last_own, guest_own, last_sib, guest_sib)):
        late[pl.ds(n * most, most)] = source[...]
    count = count_of(table, 0, blocks, 1)

    def write(n):
        return pltpu.make_async_copy(late.at[table[n, 2]], image.at[table[n, 1]], out_sems.at[n])

    def add(n, totals):
        write(n).start()
        value, found = wave[table[n, 1]].astype(jnp.float32), late[table[n, 2]]
        return totals[0] + folded(value * value), totals[1] + folded(value * found)

    norm_map, correlation_map = lax.fori_loop(0, count, add, (zero, zero))
    norm = jnp.sum(norm_map, keepdims=True)
    correlation = jnp.sum(correlation_map, keepdims=True)
    ratio = ratio_of(norm, correlation)

    def rest(n, total):
        residual = late[table[n, 2]] - ratio * wave[table[n, 1]].astype(jnp.float32)
        return total + folded(residual * residual)

    resid = jnp.sum(lax.fori_loop(0, count, rest, zero), keepdims=True)
    first = [sums_first[n : n + 1, 0:1] for n in range(3)]
    sums[...] = lined(*merged(first, (norm, correlation, resid)))

    @pl.loop(0, count)
    def _(n):
        write(n).wait()


def correction_kernel(
    entries, sums, near, far, across, image_in, wave_in, out, ratio, image, wave, result, sems
):
    chunks = sems.shape[1]
    size = image.shape[0] // chunks

    def copy(kind, source, target, n):
        part = pl.ds(n * size, size)
        return pltpu.make_async_copy(source.at[part], target.at[part], sems.at[kind, n])

    images = [copy(0, image_in, image, n) for n in range(chunks)]
    waves = [copy(1, wave_in, wave, n) for n in range(chunks)]
    results = [copy(2, result, out, n) for n in range(chunks)]
    for n in range(chunks):
        images[n].start()
        waves[n].start()

    def total(ref):
        return merged(*([ref[base + n : base + n + 1, 0:1] for n in range(3)] for base in (0, 8)))

    whole = merged(merged(total(sums), total(near)), merged(total(far), total(across)))
    rayleigh = whole[1] / whole[0]
    scale = lax.rsqrt(whole[2] / entries + 1e-06)
    ratio[...] = jnp.broadcast_to(rayleigh, (8, 128))
    for n in range(chunks):
        images[n].wait()
        waves[n].wait()
        part = pl.ds(n * size, size)
        result[part] = (image[part] - rayleigh * wave[part].astype(jnp.float32)) * scale
        results[n].start()
    for n in range(chunks):
        results[n].wait()


def ratio_of(norm, correlation):
    return jnp.where(norm > 0, correlation / jnp.where(norm > 0, norm, 1.0), 0.0)


def merged(one, two):
    low, high = jnp.minimum(one[0], two[0]), jnp.maximum(one[0], two[0])
    norm = one[0] + two[0]
    gap = ratio_of(one[0], one[1]) - ratio_of(two[0], two[1])
    shared = low * jnp.where(norm > 0, high / jnp.where(norm > 0, norm, 1.0), 0.0)
    return norm, one[1] + two[1], one[2] + two[2] + gap * gap * shared


def ranks(key):
    at = jnp.arange(key.shape[-1])
    mine, others = key[..., :, None], key[..., None, :]
    before = (others < mine) | ((others == mine) & (at[None, :] < at[:, None]))
    return jnp.sum(before.astype(jnp.int32), axis=-1)


def call(kernel, out_shape, in_spaces, out_spaces, scratch, flops=1, aliases={}):
    return pl.pallas_call(
        kernel,
        out_shape=out_shape,
        in_specs=[pl.BlockSpec(memory_space=space) for space in in_spaces],
        out_specs=jax.tree.map(lambda space: pl.BlockSpec(memory_space=space), out_spaces),
        scratch_shapes=scratch,
        input_output_aliases=aliases,
        compiler_params=pltpu.CompilerParams(vmem_limit_bytes=VMEM_LIMIT),
        cost_estimate=pl.CostEstimate(
            flops=flops, bytes_accessed=1, transcendentals=0
        ),
    )


def after(array, *others):
    return lax.optimization_barrier((array, *others))[0]


def on_device(
    wavefunction,
    left_sector,
    right_sector,
    phys_index,
    left_environment,
    right_environment,
    term_weights,
):
    blocks, dim, _ = wavefunction.shape
    terms, per_device = left_environment.shape[:2]
    most = 2 * max(1, blocks // 8)
    first_slots = blocks - most
    index = lax.axis_index("sector")
    z, y, c = index // 2, index % 2, lax.axis_index("term")
    flags = jnp.stack([z < 2, y != c, y == c]).astype(jnp.int32)

    def hop(array, step, where=lambda z, y, c: True):
        return move(array, pairs_of(step, where))

    def mine_of(own, swapped):
        return jnp.where(y == c, own, swapped)

    def tiled(facts):
        rows, columns = facts.shape
        return jnp.pad(facts.astype(bf16), ((0, dim - rows), (0, dim - columns)))[None]

    HBM, VMEM, SMEM = pltpu.HBM, pltpu.VMEM, pltpu.SMEM
    bf16, f32 = jnp.bfloat16, jnp.float32
    square = (dim, dim)
    env = (terms, per_device) + square
    info = jnp.stack([left_sector, right_sector - index * per_device, phys_index])
    parity = jnp.stack([c, c, 1 - c])[:, None]
    side = jnp.where(jnp.arange(2) == 0, y, 1 - y)

    def sorted_out(infos, count):
        left_device = infos[:, 0] // per_device
        step = left_device // 2 - z
        stage = jnp.where(step == 0, 0, jnp.where(step == -1, 1, jnp.where(step == 1, 2, 3)))
        here = left_device % 2 == parity[:count]
        guest = here & (jnp.abs(step) == 3)
        stage = jnp.where(here & ~guest, stage, -1)
        place = ranks(jnp.where(stage < 0, 0, jnp.where(stage == 3, 2, 1)))
        return here, guest, stage, place

    def ordered(places, rows, fields):
        chosen = (jnp.arange(rows)[None, :, None] == places[:, None, :]).astype(f32)
        values = jnp.stack(fields, axis=-1).astype(f32)
        return jnp.einsum("rsk,rkf->rsf", chosen, values, precision=lax.Precision.HIGHEST).astype(
            jnp.int32
        )

    weights_sib = move(term_weights, CORE)
    left_n = move(left_environment, DIAGONAL)
    left_n, weights_sib = lax.optimization_barrier((left_n, weights_sib))
    weights = mine_of(term_weights, weights_sib).astype(f32).T
    weights = jnp.broadcast_to(weights[:, :, None], weights.shape + (dim,)).reshape(-1, terms * dim)
    left_mine = mine_of(left_environment, left_n)
    below = hop(left_mine, up)
    above = hop(left_mine, down)

    right_n = move(after(right_environment, left_mine), DIAGONAL)
    right_mine = mine_of(right_environment, right_n)
    info_other = move(after(info, left_mine), COLUMN)

    block = jnp.arange(blocks)
    _, guest, _, _ = sorted_out(info[None], 1)
    guest_place = ranks(jnp.where(guest, 0, 1))
    guest_fields = [jnp.where(guest, 3, -1), block[None], info[None, 0] % per_device]
    guest_fields += [jnp.broadcast_to(side[:1, None] != c, (1, blocks)), info[None, 1], info[None, 2]]
    guest_table = ordered(guest_place, most, guest_fields)[0]
    picked = call(
        pick_kernel,
        jax.ShapeDtypeStruct((most + 1,) + square, bf16),
        [SMEM, VMEM, VMEM],
        VMEM,
        [],
    )(guest_table, wavefunction, tiled(guest_table))
    wave_guest = move(after(picked, left_mine), GUEST)

    infos = jnp.stack([info, info_other, info])
    here, guest, stage, place = sorted_out(infos, 3)
    guest_place = ranks(jnp.where(guest, 0, 1))
    table = ordered(
        place[:2],
        blocks,
        [
            stage[:2],
            jnp.broadcast_to(block, (2, blocks)),
            infos[:2, 0] % per_device,
            jnp.broadcast_to(side[:, None] != c, (2, blocks)),
            infos[:2, 1],
            infos[:2, 2],
        ],
    )
    far_table = table[:, first_slots:].reshape(2 * most, -1)
    table = table.reshape(2 * blocks, -1)
    table = table.reshape(2, blocks, -1)

    def source_of(which, of):
        code = jnp.where(guest[of], 2, jnp.where(place[of] < first_slots, 0, 1))
        slot = jnp.where(
            guest[of], guest_place[of], jnp.where(place[of] < first_slots, place[of], place[of] - first_slots)
        )
        return jnp.stack([code + 3 * which, slot], axis=-1)

    sources = jnp.where(here[0][:, None], source_of(0, 0), source_of(1, 2))
    is_late = sources[:, 0] % 3 != 0
    late_order = ranks(jnp.where(is_late, 0, 1)[None])
    source_row = (sources[:, 0] - sources[:, 0] // 3 - 1) * most + sources[:, 1]
    late_table = ordered(late_order, blocks, [is_late[None], block[None], source_row[None]])[0]

    held = (below, above, right_mine, wave_guest)
    held += (table, far_table, weights, sources, late_table)
    held = lax.optimization_barrier(held)
    below, above, right_mine, wave_guest = held[:4]
    table, far_table, weights, sources, late_table = held[4:]
    below_two = hop(below, up, inner)
    above_two = hop(above, down, inner)
    right_guest = hop(right_mine, inward, outer)
    wave_other = move(after(wavefunction, right_mine), COLUMN)
    right_sib = move(right_mine, CORE)
    def near(relation, blocks_of, kind):
        return call(
            near_kernel,
            (
                jax.ShapeDtypeStruct((first_slots,) + square, kind),
                jax.ShapeDtypeStruct((most,) + square, kind),
                jax.ShapeDtypeStruct((most, dim, terms * dim), bf16),
            ),
            [SMEM, VMEM] + [HBM] * 6,
            (HBM, VMEM, HBM),
            [
                pltpu.VMEM((blocks,) + square, kind),
                pltpu.VMEM((most, dim, terms * dim), bf16),
                pltpu.VMEM((blocks,) + square, bf16),
                pltpu.VMEM((2,) + env, bf16),
                pltpu.VMEM((3,) + env, bf16),
                pltpu.SemaphoreType.DMA((7,)),
                pltpu.SemaphoreType.DMA((most,)),
            ],
        )(
            table[relation], weights, blocks_of, right_mine, right_sib,
            left_mine, below, above,
        )

    own, own_last, carried_own = near(0, wavefunction, f32)
    other, other_last, carried_other = near(1, wave_other, bf16)
    wave_guest_other = move(after(wave_guest, own), COLUMN_INNER)
    held = (below_two, above_two, right_guest, wave_guest_other)
    held += (own, own_last, carried_own, other, other_last, carried_other)
    held = lax.optimization_barrier(held)
    below_two, above_two, right_guest, wave_guest_other = held[:4]
    own, own_last, carried_own, other, other_last, carried_other = held[4:]
    first_got = move(other, COLUMN)
    right_guest_sib = hop(right_guest, other_core, inner)
    guest_got = jnp.concatenate(
        [guests[most, :most, :6] for guests in (wave_guest, wave_guest_other)]
    ).astype(jnp.int32)

    last = jax.ShapeDtypeStruct((most,) + square, f32)
    last_sent = jax.ShapeDtypeStruct((most,) + square, bf16)
    last_own, last_other, guest_own, guest_other = call(
        far_kernel,
        (last, last_sent, last_sent, last_sent),
        [SMEM] * 3 + [VMEM] + [HBM] * 4 + [VMEM] * 2 + [HBM] * 4,
        (VMEM,) * 4,
        [
            pltpu.VMEM((2 * most, dim, terms * dim), bf16),
            pltpu.VMEM((2 * most, dim, terms * dim), bf16),
            pltpu.VMEM((2 * most,) + square, bf16),
            pltpu.VMEM((2 * most, terms) + square, bf16),
            pltpu.VMEM(env, bf16),
            pltpu.SemaphoreType.DMA((2 * most,)),
            pltpu.SemaphoreType.DMA((2 * most,)),
            pltpu.SemaphoreType.DMA((2,)),
            pltpu.SemaphoreType.DMA((1,)),
        ],
    )(
        flags, far_table, guest_got, weights, carried_own, carried_other,
        below_two, above_two, own_last, other_last,
        wave_guest, wave_guest_other, right_guest, right_guest_sib,
    )
    guest_straight = move(guest_own, GUEST_BACK)
    guest_crossed = move(guest_other, GUEST_BACK_CROSSED)
    last_got = move(last_other, COLUMN)
    last_full = last_own + last_got.astype(f32)
    first_own = own + after(first_got, last_own).astype(f32)
    first_sib = move(first_own, CORE)
    last_sib = move(last_full, CORE)
    image_shape = jax.ShapeDtypeStruct((blocks,) + square, f32)
    image, sums_first = call(
        first_kernel,
        (image_shape, jax.ShapeDtypeStruct((8, 128), f32)),
        [SMEM] + [VMEM] * 3,
        (VMEM, VMEM),
        [],
    )(after(sources, last_own), first_own, first_sib, wavefunction)
    guest_full = call(sum_kernel, last, [VMEM] * 2, VMEM, [], 2**37)(
        after(guest_straight, sums_first), guest_crossed
    )
    guest_sib = move(guest_full, CORE)

    image, sums = call(
        last_kernel,
        (image_shape, jax.ShapeDtypeStruct((8, 128), f32)),
        [SMEM] + [VMEM] * 6 + [HBM],
        (HBM, VMEM),
        [
            pltpu.VMEM((4 * most,) + square, f32),
            pltpu.SemaphoreType.DMA((blocks,)),
        ],
        aliases={7: 0},
    )(late_table, sums_first, last_full, guest_full, last_sib, guest_sib, wavefunction, image)
    sums = jnp.concatenate([sums, move(sums, COLUMN)])
    sums = [sums] + [move(sums, pairs_of(lambda z, y, c: (z ^ n, y, c))) for n in (1, 2, 3)]
    correction, rayleigh = call(
        functools.partial(correction_kernel, blocks * 8 * dim * dim),
        (image_shape, jax.ShapeDtypeStruct((8, 128), f32)),
        [VMEM] * 4 + [HBM] * 2,
        (HBM, VMEM),
        [
            pltpu.VMEM((blocks,) + square, f32),
            pltpu.VMEM((blocks,) + square, bf16),
            pltpu.VMEM((blocks,) + square, f32),
            pltpu.SemaphoreType.DMA((3, 4)),
        ],
    )(*sums, image, wavefunction)
    return image, correction, rayleigh[0, :1]


def solution(mesh):
    placed = (
        P(("parts", "sector"), None, None),
        P(("parts", "sector")),
        P(("parts", "sector")),
        P(("parts", "sector")),
        P(("parts", "term"), "sector", None, None),
        P(("parts", "term"), "sector", None, None),
        P(("parts", "term"), None),
    )
    paired = mesh.shape["sector"] == 8 and mesh.shape["term"] == 2
    return jax.shard_map(
        on_device if paired else on_device_any,
        mesh=mesh,
        in_specs=placed,
        out_specs=(
            P(("parts", "sector"), None, None),
            P(("parts", "sector"), None, None),
            P("parts"),
        ),
        check_vma=False,
    )
```

```python
import functools

import jax
import jax.numpy as jnp
from jax import lax
from jax.experimental import pallas as pl
from jax.experimental.pallas import tpu as pltpu
from jax.sharding import PartitionSpec as P

BOTH = ("sector", "term")
VMEM_LIMIT = 60 * 2**20
VMEM_SMALL = 32 * 2**20


def on_device_any(
    wavefunction,
    left_sector,
    right_sector,
    phys_index,
    left_environment,
    right_environment,
    term_weights,
):
    blocks = wavefunction.shape[0]
    sector_dim = wavefunction.shape[1]
    sector_count = lax.axis_size("sector")
    per_device = right_environment.shape[1]
    capacity = 2 * max(1, blocks // sector_count)
    own_index = lax.axis_index("sector")
    right_local = right_sector - own_index * per_device
    target = left_sector // per_device
    positions = jnp.arange(blocks)
    earlier = (target[None, :] == target[:, None]) & (positions[None, :] < positions[:, None])
    placement_order = jnp.sum(earlier.astype(jnp.int32), axis=1)
    physical_selector_matrix = (
        phys_index[:, None] == jnp.arange(term_weights.shape[1])[None, :]
    ).astype(jnp.bfloat16)
    slot_index = target * capacity + placement_order
    slot_count = sector_count * capacity
    selector_f = (jnp.arange(slot_count)[:, None] == slot_index[None, :]).astype(jnp.float32)
    wanted = jnp.dot(
        selector_f, (left_sector % per_device).astype(jnp.float32), precision=lax.Precision.HIGHEST
    ).astype(jnp.int32)
    requests = lax.all_to_all(
        wanted.reshape(sector_count, capacity), "sector", split_axis=0, concat_axis=0, tiled=True
    )
    picked = jnp.take(left_environment, requests.reshape(-1), axis=1)
    picked = jnp.moveaxis(picked, 0, 1).reshape(
        sector_count, capacity, left_environment.shape[0], sector_dim, sector_dim
    )
    fetched = lax.all_to_all(picked, "sector", split_axis=0, concat_axis=0, tiled=True)
    left_blocks = jnp.take(
        fetched.reshape(slot_count, left_environment.shape[0], sector_dim, sector_dim),
        slot_index,
        axis=0,
    )
    right_taken = jnp.take(right_environment, right_local, axis=1)
    block_weights = jnp.dot(
        physical_selector_matrix, term_weights.T, preferred_element_type=jnp.float32
    )
    environment_product = jnp.einsum(
        "kab,tkcb->ktac", wavefunction, right_taken, preferred_element_type=jnp.float32
    )
    carried = (environment_product * block_weights[:, :, None, None]).astype(jnp.bfloat16)
    image_partial_result = jnp.einsum(
        "ktij,ktjc->kic", left_blocks, carried, preferred_element_type=jnp.float32
    )
    image = lax.psum(image_partial_result, "term")
    wave_f32 = wavefunction.astype(jnp.float32)
    norm_wave = jnp.sum(wave_f32 * wave_f32)
    correlation = jnp.sum(wave_f32 * image)
    entries = blocks * sector_count * sector_dim * sector_dim
    norm_all, correlation_all = lax.psum((norm_wave, correlation), "sector")
    rayleigh = correlation_all / norm_all
    residual = image - rayleigh * wave_f32
    norm_resid = lax.psum(jnp.sum(residual * residual), "sector")
    correction = residual * lax.rsqrt(norm_resid / entries + 1e-06)
    return (image, correction, jnp.reshape(rayleigh, (1,)))


def pairs_of(target, chosen=lambda z, y, c: True):
    found = []
    for z in range(4):
        for y in range(2):
            for c in range(2):
                if chosen(z, y, c):
                    to = target(z, y, c)
                    if 0 <= to[0] < 4:
                        found.append(((z * 2 + y) * 2 + c, (to[0] * 2 + to[1]) * 2 + to[2]))
    return found


def inner(z, y, c):
    return z in (1, 2)


def outer(z, y, c):
    return z in (0, 3)


def straight(z, y, c):
    return y == c


def crossed(z, y, c):
    return y != c


def both(one, two):
    return lambda z, y, c: one(z, y, c) and two(z, y, c)


def up(z, y, c):
    return z + 1, y, c


def down(z, y, c):
    return z - 1, y, c


def other_core(z, y, c):
    return z, y, 1 - c


def other_column(z, y, c):
    return z, 1 - y, c


def inward(z, y, c):
    return (1 if z == 0 else 2), y, c


def outward(z, y, c):
    return (0 if z == 1 else 3), y, c


def outward_crossed(z, y, c):
    return (0 if z == 1 else 3), 1 - y, c


DIAGONAL = pairs_of(lambda z, y, c: (z, 1 - y, 1 - c), crossed)
CORE = pairs_of(other_core)
COLUMN = pairs_of(other_column)
COLUMN_INNER = pairs_of(other_column, inner)
GUEST = pairs_of(inward, outer)
GUEST_BACK = pairs_of(outward, inner)
GUEST_BACK_CROSSED = pairs_of(outward_crossed, inner)


def move(array, pairs):
    return lax.ppermute(array, BOTH, pairs)


def carried_of(wave, right, weights):
    terms, dim, _ = right.shape
    product = lax.dot_general(
        wave,
        right.reshape(terms * dim, dim),
        (((1,), (1,)), ((), ())),
        preferred_element_type=jnp.float32,
    )
    return (product * weights).astype(jnp.bfloat16)


def applied(left, carried):
    terms, dim, _ = left.shape
    lefts = jnp.concatenate([left[t] for t in range(terms)], axis=1)
    stacked = jnp.concatenate(
        [carried[:, t * dim : (t + 1) * dim] for t in range(terms)], axis=0
    )
    return jnp.dot(lefts, stacked, preferred_element_type=jnp.float32)


def choose(flag, one, two, target, sem):
    @pl.when(flag)
    def _():
        pltpu.make_async_copy(one, target, sem).start()

    @pl.when(jnp.logical_not(flag))
    def _():
        pltpu.make_async_copy(two, target, sem).start()


def grouped(low, high, step, body):
    @pl.loop(0, (high - low + step - 1) // step)
    def _(group):
        for n in range(step):
            body(jnp.minimum(low + group * step + n, high - 1))


def count_of(table, base, rows, stage):
    def add(row, total):
        return total + (table[base + row, 0] == stage).astype(jnp.int32)

    return lax.fori_loop(0, rows, add, jnp.int32(0))


def near_kernel(
    table, weights, wave_in, right_mine, right_sib, left_mine, below, above,
    first, last, carried_out,
    result, carried, wave, right, left, sems, carried_sems,
):
    blocks = wave.shape[0]
    most = last.shape[0]
    first_slots = blocks - most
    copies = [
        pltpu.make_async_copy(source, target, sems.at[n])
        for n, (source, target) in enumerate(
            (
                (wave_in, wave),
                (right_mine, right.at[0]),
                (right_sib, right.at[1]),
                (left_mine, left.at[0]),
                (below, left.at[1]),
                (above, left.at[2]),
            )
        )
    ]
    for copy in copies:
        copy.start()
    result[...] = jnp.zeros_like(result)
    skipped = count_of(table, 0, blocks, -1)
    end = blocks - count_of(table, 0, blocks, 3)
    for copy in copies[:3]:
        copy.wait()

    def carry(slot):
        return carried_of(
            wave[table[slot, 1]], right[table[slot, 3], :, table[slot, 4]], weights[pl.ds(table[slot, 5], 1), :]
        )

    def written(slot):
        at = slot - first_slots
        return pltpu.make_async_copy(carried.at[at], carried_out.at[at], carried_sems.at[at])

    def keep(slot):
        carried[slot - first_slots] = carry(slot)

    grouped(end, blocks, 4, keep)

    @pl.loop(end, blocks)
    def _(slot):
        written(slot).start()

    for copy in copies[3:]:
        copy.wait()

    def apply(slot):
        found = applied(left[table[slot, 0], :, table[slot, 2]], carry(slot))
        result[slot] = found.astype(result.dtype)

    grouped(skipped, end, 4, apply)
    outs = [
        pltpu.make_async_copy(result.at[part], target, sems.at[len(copies) + n])
        for n, (part, target) in enumerate(
            ((pl.ds(0, first_slots), first), (pl.ds(first_slots, most), last))
        )
    ]
    for out in outs:
        out.start()
    for out in outs:
        out.wait()

    @pl.loop(end, blocks)
    def _(slot):
        written(slot).wait()


def guest_kernel(
    flags, table, weights, below, above, wave_own, wave_other, right_mine, right_sib,
    own_out, other_out,
    wave, right, left, sems,
):
    half = own_out.shape[0]
    counts = [count_of(table, part * half, half, 3) for part in range(2)]
    copies = [
        pltpu.make_async_copy(source, target, sems.at[n])
        for n, (source, target) in enumerate(
            (
                (right_mine, right.at[0]),
                (right_sib, right.at[1]),
                (wave_own.at[pl.ds(0, half)], wave.at[pl.ds(0, half)]),
                (wave_other.at[pl.ds(0, half)], wave.at[pl.ds(half, half)]),
            )
        )
    ]

    @pl.when(counts[0] + counts[1] > 0)
    def _():
        for copy in copies:
            copy.start()
        choose(flags[0] == 1, above, below, left, sems.at[len(copies)])

    own_out[...] = jnp.zeros_like(own_out)
    other_out[...] = jnp.zeros_like(other_out)

    @pl.when(counts[0] + counts[1] > 0)
    def _():
        for copy in copies:
            copy.wait()
        pltpu.make_async_copy(above, left, sems.at[len(copies)]).wait()

    for part, target in enumerate((own_out, other_out)):

        def apply(row):
            carried = carried_of(
                wave[row],
                right[flags[1 + part], :, table[row, 4]],
                weights[pl.ds(table[row, 5], 1), :],
            )
            result = applied(left[:, table[row, 2]], carried)
            target[row - part * half] = result.astype(target.dtype)

        grouped(part * half, part * half + counts[part], 4, apply)


def far_kernel(
    flags, table, carried_own, carried_other, below, above, own, other,
    own_out, other_out,
    held, left, sems, more_sems,
):
    half = own_out.shape[0]
    lows = [half - count_of(table, part * half, half, 3) for part in range(2)]
    choose(flags[0] == 1, above, below, left, more_sems.at[0])
    kept = [
        pltpu.make_async_copy(source, target, more_sems.at[1 + n])
        for n, (source, target) in enumerate(((own, own_out), (other, other_out)))
    ]
    for copy in kept:
        copy.start()
    for part, carried in enumerate((carried_own, carried_other)):

        @pl.loop(lows[part], half)
        def _(slot):
            row = part * half + slot
            pltpu.make_async_copy(carried.at[slot], held.at[row], sems.at[row]).start()

    for copy in kept:
        copy.wait()
    pltpu.make_async_copy(above, left, more_sems.at[0]).wait()
    for part, (carried, target) in enumerate(((carried_other, other_out), (carried_own, own_out))):
        part = 1 - part

        @pl.loop(lows[part], half)
        def _(slot):
            row = part * half + slot
            pltpu.make_async_copy(carried.at[slot], held.at[row], sems.at[row]).wait()

        def apply(slot):
            row = part * half + slot
            target[slot] = applied(left[:, table[row, 2]], held[row]).astype(target.dtype)

        grouped(lows[part], half, 4, apply)


def pick_kernel(table, own, facts, out):
    slots = out.shape[0] - 1
    out[slots] = facts[0]

    @pl.loop(0, slots)
    def _(slot):
        out[slot] = own[table[slot, 1]]


def folded(value):
    return jnp.sum(value.reshape(-1, 8, 128), axis=0)


def first_kernel(table, own, got, wave, whole, sums):
    blocks = wave.shape[0]
    zero = jnp.zeros((8, 128), jnp.float32)
    whole[...] = own[...] + got[...].astype(jnp.float32)
    count = count_of(table, 0, blocks, 1)

    def add(n, totals):
        value, found = wave[table[n, 1]].astype(jnp.float32), whole[table[n, 2]]
        return totals[0] + folded(value * value), totals[1] + folded(value * found)

    norm_map, correlation_map = lax.fori_loop(0, count, add, (zero, zero))
    norm = jnp.sum(norm_map, keepdims=True)
    correlation = jnp.sum(correlation_map, keepdims=True)
    ratio = ratio_of(norm, correlation)

    def rest(n, total):
        residual = whole[table[n, 2]] - ratio * wave[table[n, 1]].astype(jnp.float32)
        return total + folded(residual * residual)

    resid = jnp.sum(lax.fori_loop(0, count, rest, zero), keepdims=True)
    sums[...] = lined(norm, correlation, resid)


def lined(*values):
    line = lax.broadcasted_iota(jnp.int32, (8, 128), 0)
    result = jnp.zeros((8, 128), jnp.float32)
    for n, value in enumerate(values):
        result = jnp.where(line == n, value, result)
    return result


def sum_kernel(one, two, out):
    out[...] = one[...].astype(out.dtype) + two[...].astype(out.dtype)


def late_kernel(table, sums_first, last_own, last_got, guest_full, wave, late, sums):
    blocks = wave.shape[0]
    most = last_own.shape[0]
    zero = jnp.zeros((8, 128), jnp.float32)
    late[pl.ds(0, most)] = last_own[...] + last_got[...].astype(jnp.float32)
    late[pl.ds(most, most)] = guest_full[...]
    count = count_of(table, 0, blocks, 1)

    def add(n, totals):
        value, found = wave[table[n, 1]].astype(jnp.float32), late[table[n, 2]]
        return totals[0] + folded(value * value), totals[1] + folded(value * found)

    norm_map, correlation_map = lax.fori_loop(0, count, add, (zero, zero))
    norm = jnp.sum(norm_map, keepdims=True)
    correlation = jnp.sum(correlation_map, keepdims=True)
    ratio = ratio_of(norm, correlation)

    def rest(n, total):
        residual = late[table[n, 2]] - ratio * wave[table[n, 1]].astype(jnp.float32)
        return total + folded(residual * residual)

    resid = jnp.sum(lax.fori_loop(0, count, rest, zero), keepdims=True)
    first = [sums_first[n : n + 1, 0:1] for n in range(3)]
    sums[...] = lined(*merged(first, (norm, correlation, resid)))


def place_kernel(table, first_own, late_own, first_sib, late_sib, image, kept, sem):
    @pl.loop(0, kept.shape[0])
    def _(k):
        for code, source in enumerate((first_own, late_own, first_sib, late_sib)):

            @pl.when(table[k, 0] == code)
            def _():
                kept[k] = source[table[k, 1]]

    copy = pltpu.make_async_copy(kept, image, sem.at[0])
    copy.start()
    copy.wait()


def correction_kernel(entries, sums, near, far, across, image, wave, out, ratio, result, sems):
    chunks = sems.shape[0]
    size = image.shape[0] // chunks

    def total(ref):
        parts = [[ref[base + n : base + n + 1, 0:1] for n in range(3)] for base in (0, 8, 16, 24)]
        return merged(merged(*parts[:2]), merged(*parts[2:]))

    whole = merged(merged(total(sums), total(near)), merged(total(far), total(across)))
    rayleigh = whole[1] / whole[0]
    scale = lax.rsqrt(whole[2] / entries + 1e-06)
    ratio[0] = rayleigh[0, 0]
    copies = []
    for n in range(chunks):
        part = pl.ds(n * size, size)
        result[part] = (image[part] - rayleigh * wave[part].astype(jnp.float32)) * scale
        copies.append(pltpu.make_async_copy(result.at[part], out.at[part], sems.at[n]))
        copies[n].start()
    for copy in copies:
        copy.wait()


def ratio_of(norm, correlation):
    return jnp.where(norm > 0, correlation / jnp.where(norm > 0, norm, 1.0), 0.0)


def merged(one, two):
    low, high = jnp.minimum(one[0], two[0]), jnp.maximum(one[0], two[0])
    norm = one[0] + two[0]
    gap = ratio_of(one[0], one[1]) - ratio_of(two[0], two[1])
    shared = low * jnp.where(norm > 0, high / jnp.where(norm > 0, norm, 1.0), 0.0)
    return norm, one[1] + two[1], one[2] + two[2] + gap * gap * shared


def ranks(key):
    at = jnp.arange(key.shape[-1])
    mine, others = key[..., :, None], key[..., None, :]
    before = (others < mine) | ((others == mine) & (at[None, :] < at[:, None]))
    return jnp.sum(before.astype(jnp.int32), axis=-1)


def call(kernel, out_shape, in_spaces, out_spaces, scratch, flops=1, aliases={}, vmem=VMEM_LIMIT):
    return pl.pallas_call(
        kernel,
        out_shape=out_shape,
        in_specs=[pl.BlockSpec(memory_space=space) for space in in_spaces],
        out_specs=jax.tree.map(lambda space: pl.BlockSpec(memory_space=space), out_spaces),
        scratch_shapes=scratch,
        input_output_aliases=aliases,
        compiler_params=pltpu.CompilerParams(vmem_limit_bytes=vmem),
        cost_estimate=pl.CostEstimate(
            flops=flops, bytes_accessed=1, transcendentals=0
        ),
    )


def after(array, *others):
    return lax.optimization_barrier((array, *others))[0]


def on_device(
    wavefunction,
    left_sector,
    right_sector,
    phys_index,
    left_environment,
    right_environment,
    term_weights,
):
    blocks, dim, _ = wavefunction.shape
    terms, per_device = left_environment.shape[:2]
    most = 2 * max(1, blocks // 8)
    first_slots = blocks - most
    index = lax.axis_index("sector")
    z, y, c = index // 2, index % 2, lax.axis_index("term")
    flags = jnp.stack([z < 2, y != c, y == c]).astype(jnp.int32)

    def hop(array, step, where=lambda z, y, c: True):
        return move(array, pairs_of(step, where))

    def mine_of(own, swapped):
        return jnp.where(y == c, own, swapped)

    def tiled(facts):
        rows, columns = facts.shape
        return jnp.pad(facts.astype(bf16), ((0, dim - rows), (0, dim - columns)))[None]

    HBM, VMEM, SMEM = pltpu.HBM, pltpu.VMEM, pltpu.SMEM
    bf16, f32 = jnp.bfloat16, jnp.float32
    square = (dim, dim)
    env = (terms, per_device) + square
    info = jnp.stack([left_sector, right_sector - index * per_device, phys_index])
    parity = jnp.stack([c, c, 1 - c])[:, None]
    side = jnp.where(jnp.arange(2) == 0, y, 1 - y)

    def sorted_out(infos, count):
        left_device = infos[:, 0] // per_device
        step = left_device // 2 - z
        stage = jnp.where(step == 0, 0, jnp.where(step == -1, 1, jnp.where(step == 1, 2, 3)))
        here = left_device % 2 == parity[:count]
        guest = here & (jnp.abs(step) == 3)
        stage = jnp.where(here & ~guest, stage, -1)
        place = ranks(jnp.where(stage < 0, 0, jnp.where(stage == 3, 2, 1)))
        return here, guest, stage, place

    def ordered(places, rows, fields):
        chosen = (jnp.arange(rows)[None, :, None] == places[:, None, :]).astype(f32)
        values = jnp.stack(fields, axis=-1).astype(f32)
        return jnp.einsum("rsk,rkf->rsf", chosen, values, precision=lax.Precision.HIGHEST).astype(
            jnp.int32
        )

    weights_sib = move(term_weights, CORE)
    left_n = move(left_environment, DIAGONAL)
    left_n, weights_sib = lax.optimization_barrier((left_n, weights_sib))
    weights = mine_of(term_weights, weights_sib).astype(f32).T
    weights = jnp.broadcast_to(weights[:, :, None], weights.shape + (dim,)).reshape(-1, terms * dim)
    left_mine = mine_of(left_environment, left_n)
    below = hop(left_mine, up)
    above = hop(left_mine, down)

    right_n = move(after(right_environment, left_mine), DIAGONAL)
    right_mine = mine_of(right_environment, right_n)
    info_other = move(after(info, left_mine), COLUMN)

    block = jnp.arange(blocks)
    _, guest, _, _ = sorted_out(info[None], 1)
    guest_place = ranks(jnp.where(guest, 0, 1))
    guest_fields = [jnp.where(guest, 3, -1), block[None], info[None, 0] % per_device]
    guest_fields += [jnp.broadcast_to(side[:1, None] != c, (1, blocks)), info[None, 1], info[None, 2]]
    guest_table = ordered(guest_place, most, guest_fields)[0]
    picked = call(
        pick_kernel,
        jax.ShapeDtypeStruct((most + 1,) + square, bf16),
        [SMEM, VMEM, VMEM],
        VMEM,
        [],
    )(guest_table, wavefunction, tiled(guest_table))
    wave_guest = move(after(picked, left_mine), GUEST)

    infos = jnp.stack([info, info_other, info])
    here, guest, stage, place = sorted_out(infos, 3)
    guest_place = ranks(jnp.where(guest, 0, 1))
    table = ordered(
        place[:2],
        blocks,
        [
            stage[:2],
            jnp.broadcast_to(block, (2, blocks)),
            infos[:2, 0] % per_device,
            jnp.broadcast_to(side[:, None] != c, (2, blocks)),
            infos[:2, 1],
            infos[:2, 2],
        ],
    )
    far_table = table[:, first_slots:].reshape(2 * most, -1)
    table = table.reshape(2 * blocks, -1)
    table = table.reshape(2, blocks, -1)

    def source_of(which, of):
        late_place = jnp.where(guest[of], most + guest_place[of], place[of] - first_slots)
        late = guest[of] | (place[of] >= first_slots)
        return jnp.stack(
            [2 * which + late.astype(jnp.int32), jnp.where(late, late_place, place[of])], axis=-1
        )

    sources = jnp.where(here[0][:, None], source_of(0, 0), source_of(1, 2))
    picked_out = jnp.stack([sources[:, 0] == 0, sources[:, 0] == 1]).astype(jnp.int32)
    first_table, late_table = ordered(
        ranks(1 - picked_out),
        blocks,
        [
            picked_out,
            jnp.broadcast_to(block, (2, blocks)),
            jnp.broadcast_to(sources[:, 1], (2, blocks)),
        ],
    )

    held = (below, above, right_mine, wave_guest)
    held += (table, far_table, weights, sources, first_table, late_table)
    held = lax.optimization_barrier(held)
    below, above, right_mine, wave_guest = held[:4]
    table, far_table, weights, sources, first_table, late_table = held[4:]
    below_two = hop(below, up, inner)
    above_two = hop(above, down, inner)
    right_guest = hop(right_mine, inward, outer)
    wave_other = move(after(wavefunction, right_mine), COLUMN)
    right_sib = move(right_mine, CORE)
    def near(relation, blocks_of, kind):
        return call(
            near_kernel,
            (
                jax.ShapeDtypeStruct((first_slots,) + square, kind),
                jax.ShapeDtypeStruct((most,) + square, kind),
                jax.ShapeDtypeStruct((most, dim, terms * dim), bf16),
            ),
            [SMEM, VMEM] + [HBM] * 6,
            (HBM, HBM, HBM),
            [
                pltpu.VMEM((blocks,) + square, kind),
                pltpu.VMEM((most, dim, terms * dim), bf16),
                pltpu.VMEM((blocks,) + square, bf16),
                pltpu.VMEM((2,) + env, bf16),
                pltpu.VMEM((3,) + env, bf16),
                pltpu.SemaphoreType.DMA((8,)),
                pltpu.SemaphoreType.DMA((most,)),
            ],
        )(
            table[relation], weights, blocks_of, right_mine, right_sib,
            left_mine, below, above,
        )

    own, own_last, carried_own = near(0, wavefunction, f32)
    other, other_last, carried_other = near(1, wave_other, bf16)
    wave_guest_other = move(after(wave_guest, own), COLUMN_INNER)
    held = (below_two, above_two, right_guest, wave_guest_other)
    held += (own, own_last, carried_own, other, other_last, carried_other)
    held = lax.optimization_barrier(held)
    below_two, above_two, right_guest, wave_guest_other = held[:4]
    own, own_last, carried_own, other, other_last, carried_other = held[4:]
    first_got = move(other, COLUMN)
    right_guest_sib = hop(right_guest, other_core, inner)
    guest_got = jnp.concatenate(
        [guests[most, :most, :6] for guests in (wave_guest, wave_guest_other)]
    ).astype(jnp.int32)

    last = jax.ShapeDtypeStruct((most,) + square, f32)
    last_sent = jax.ShapeDtypeStruct((most,) + square, bf16)
    guest_own, guest_other = call(
        guest_kernel,
        (last_sent, last_sent),
        [SMEM] * 2 + [VMEM] + [HBM] * 6,
        (VMEM,) * 2,
        [
            pltpu.VMEM((2 * most,) + square, bf16),
            pltpu.VMEM((2,) + env, bf16),
            pltpu.VMEM(env, bf16),
            pltpu.SemaphoreType.DMA((5,)),
        ],
    )(
        flags, guest_got, weights, below_two, above_two,
        wave_guest, wave_guest_other, right_guest, right_guest_sib,
    )
    guest_straight = move(guest_own, GUEST_BACK)
    guest_crossed = move(guest_other, GUEST_BACK_CROSSED)
    last_own, last_other = call(
        far_kernel,
        (last, last_sent),
        [SMEM] * 2 + [HBM] * 6,
        (VMEM,) * 2,
        [
            pltpu.VMEM((2 * most, dim, terms * dim), bf16),
            pltpu.VMEM(env, bf16),
            pltpu.SemaphoreType.DMA((2 * most,)),
            pltpu.SemaphoreType.DMA((3,)),
        ],
        2**37,
    )(
        flags, after(far_table, guest_own), carried_own, carried_other, below_two, above_two,
        own_last, other_last,
    )
    last_got = move(last_other, COLUMN)
    first_own, sums_first = call(
        first_kernel,
        (jax.ShapeDtypeStruct((first_slots,) + square, f32), jax.ShapeDtypeStruct((8, 128), f32)),
        [SMEM] + [VMEM] * 3,
        (VMEM, VMEM),
        [],
        vmem=VMEM_SMALL,
    )(first_table, own, after(first_got, last_own), wavefunction)
    first_sib = move(first_own, CORE)
    guest_full = call(sum_kernel, last, [VMEM] * 2, VMEM, [], 2**37, vmem=VMEM_SMALL)(
        after(guest_straight, sums_first), guest_crossed
    )
    late, sums = call(
        late_kernel,
        (jax.ShapeDtypeStruct((2 * most,) + square, f32), jax.ShapeDtypeStruct((8, 128), f32)),
        [SMEM] + [VMEM] * 5,
        (VMEM, VMEM),
        [],
        vmem=VMEM_SMALL,
    )(late_table, sums_first, last_own, last_got, guest_full, wavefunction)
    late_sib = move(late, CORE)
    image_shape = jax.ShapeDtypeStruct((blocks,) + square, f32)
    image, kept = call(
        place_kernel,
        (image_shape, image_shape),
        [SMEM] + [VMEM] * 4,
        (HBM, VMEM),
        [pltpu.SemaphoreType.DMA((1,))],
        vmem=VMEM_SMALL,
    )(sources, first_own, late, first_sib, late_sib)
    for pairs in (CORE, COLUMN):
        sums = jnp.concatenate([sums, move(sums, pairs)])
    sums = [sums] + [move(sums, pairs_of(lambda z, y, c: (z ^ n, y, c))) for n in (1, 2, 3)]
    correction, rayleigh = call(
        functools.partial(correction_kernel, blocks * 8 * dim * dim),
        (image_shape, jax.ShapeDtypeStruct((1,), f32)),
        [VMEM] * 6,
        (HBM, SMEM),
        [pltpu.VMEM((blocks,) + square, f32), pltpu.SemaphoreType.DMA((8,))],
        vmem=VMEM_SMALL,
    )(*sums, kept, wavefunction)
    return image, correction, rayleigh


def solution(mesh):
    placed = (
        P(("parts", "sector"), None, None),
        P(("parts", "sector")),
        P(("parts", "sector")),
        P(("parts", "sector")),
        P(("parts", "term"), "sector", None, None),
        P(("parts", "term"), "sector", None, None),
        P(("parts", "term"), None),
    )
    paired = mesh.shape["sector"] == 8 and mesh.shape["term"] == 2
    return jax.shard_map(
        on_device if paired else on_device_any,
        mesh=mesh,
        in_specs=placed,
        out_specs=(
            P(("parts", "sector"), None, None),
            P(("parts", "sector"), None, None),
            P("parts"),
        ),
        check_vma=False,
    )
```

```python
import functools

import jax
import jax.numpy as jnp
from jax import lax
from jax.experimental import pallas as pl
from jax.experimental.pallas import tpu as pltpu
from jax.sharding import PartitionSpec as P

BOTH = ("sector", "term")
VMEM_LIMIT = 60 * 2**20
VMEM_SMALL = 32 * 2**20


def on_device_any(
    wavefunction,
    left_sector,
    right_sector,
    phys_index,
    left_environment,
    right_environment,
    term_weights,
):
    blocks = wavefunction.shape[0]
    sector_dim = wavefunction.shape[1]
    sector_count = lax.axis_size("sector")
    per_device = right_environment.shape[1]
    capacity = 2 * max(1, blocks // sector_count)
    own_index = lax.axis_index("sector")
    right_local = right_sector - own_index * per_device
    target = left_sector // per_device
    positions = jnp.arange(blocks)
    earlier = (target[None, :] == target[:, None]) & (positions[None, :] < positions[:, None])
    placement_order = jnp.sum(earlier.astype(jnp.int32), axis=1)
    physical_selector_matrix = (
        phys_index[:, None] == jnp.arange(term_weights.shape[1])[None, :]
    ).astype(jnp.bfloat16)
    slot_index = target * capacity + placement_order
    slot_count = sector_count * capacity
    selector_f = (jnp.arange(slot_count)[:, None] == slot_index[None, :]).astype(jnp.float32)
    wanted = jnp.dot(
        selector_f, (left_sector % per_device).astype(jnp.float32), precision=lax.Precision.HIGHEST
    ).astype(jnp.int32)
    requests = lax.all_to_all(
        wanted.reshape(sector_count, capacity), "sector", split_axis=0, concat_axis=0, tiled=True
    )
    picked = jnp.take(left_environment, requests.reshape(-1), axis=1)
    picked = jnp.moveaxis(picked, 0, 1).reshape(
        sector_count, capacity, left_environment.shape[0], sector_dim, sector_dim
    )
    fetched = lax.all_to_all(picked, "sector", split_axis=0, concat_axis=0, tiled=True)
    left_blocks = jnp.take(
        fetched.reshape(slot_count, left_environment.shape[0], sector_dim, sector_dim),
        slot_index,
        axis=0,
    )
    right_taken = jnp.take(right_environment, right_local, axis=1)
    block_weights = jnp.dot(
        physical_selector_matrix, term_weights.T, preferred_element_type=jnp.float32
    )
    environment_product = jnp.einsum(
        "kab,tkcb->ktac", wavefunction, right_taken, preferred_element_type=jnp.float32
    )
    carried = (environment_product * block_weights[:, :, None, None]).astype(jnp.bfloat16)
    image_partial_result = jnp.einsum(
        "ktij,ktjc->kic", left_blocks, carried, preferred_element_type=jnp.float32
    )
    image = lax.psum(image_partial_result, "term")
    wave_f32 = wavefunction.astype(jnp.float32)
    norm_wave = jnp.sum(wave_f32 * wave_f32)
    correlation = jnp.sum(wave_f32 * image)
    entries = blocks * sector_count * sector_dim * sector_dim
    norm_all, correlation_all = lax.psum((norm_wave, correlation), "sector")
    rayleigh = correlation_all / norm_all
    residual = image - rayleigh * wave_f32
    norm_resid = lax.psum(jnp.sum(residual * residual), "sector")
    correction = residual * lax.rsqrt(norm_resid / entries + 1e-06)
    return (image, correction, jnp.reshape(rayleigh, (1,)))


def pairs_of(target, chosen=lambda z, y, c: True):
    found = []
    for z in range(4):
        for y in range(2):
            for c in range(2):
                if chosen(z, y, c):
                    to = target(z, y, c)
                    if 0 <= to[0] < 4:
                        found.append(((z * 2 + y) * 2 + c, (to[0] * 2 + to[1]) * 2 + to[2]))
    return found


def inner(z, y, c):
    return z in (1, 2)


def outer(z, y, c):
    return z in (0, 3)


def straight(z, y, c):
    return y == c


def crossed(z, y, c):
    return y != c


def both(one, two):
    return lambda z, y, c: one(z, y, c) and two(z, y, c)


def up(z, y, c):
    return z + 1, y, c


def down(z, y, c):
    return z - 1, y, c


def other_core(z, y, c):
    return z, y, 1 - c


def other_column(z, y, c):
    return z, 1 - y, c


def inward(z, y, c):
    return (1 if z == 0 else 2), y, c


def outward(z, y, c):
    return (0 if z == 1 else 3), y, c


def outward_crossed(z, y, c):
    return (0 if z == 1 else 3), 1 - y, c


DIAGONAL = pairs_of(lambda z, y, c: (z, 1 - y, 1 - c), crossed)
CORE = pairs_of(other_core)
COLUMN = pairs_of(other_column)
ACROSS = pairs_of(lambda z, y, c: (z, 1 - y, 1 - c))
COLUMN_INNER = pairs_of(other_column, inner)
GUEST = pairs_of(inward, outer)
GUEST_BACK = pairs_of(outward, inner)
GUEST_BACK_CROSSED = pairs_of(outward_crossed, inner)


def move(array, pairs):
    return lax.ppermute(array, BOTH, pairs)


def carried_of(wave, right, weights):
    terms, dim, _ = right.shape
    product = lax.dot_general(
        wave,
        right.reshape(terms * dim, dim),
        (((1,), (1,)), ((), ())),
        preferred_element_type=jnp.float32,
    )
    return (product * weights).astype(jnp.bfloat16)


def applied(left, carried):
    terms, dim, _ = left.shape
    lefts = jnp.concatenate([left[t] for t in range(terms)], axis=1)
    stacked = jnp.concatenate(
        [carried[:, t * dim : (t + 1) * dim] for t in range(terms)], axis=0
    )
    return jnp.dot(lefts, stacked, preferred_element_type=jnp.float32)


def choose(flag, one, two, target, sem):
    @pl.when(flag)
    def _():
        pltpu.make_async_copy(one, target, sem).start()

    @pl.when(jnp.logical_not(flag))
    def _():
        pltpu.make_async_copy(two, target, sem).start()


def grouped(low, high, step, body):
    @pl.loop(0, (high - low + step - 1) // step)
    def _(group):
        for n in range(step):
            row = low + group * step + n
            body(jnp.minimum(row, high - 1), (row < high).astype(jnp.float32))


def folded(value):
    return jnp.sum(value.reshape(-1, 8, 128), axis=0)


def paired(found, wave, counted):
    return folded(found * wave.astype(jnp.float32)) * counted


def count_of(table, base, rows, stage):
    def add(row, total):
        return total + (table[base + row, 0] == stage).astype(jnp.int32)

    return lax.fori_loop(0, rows, add, jnp.int32(0))


def near_kernel(
    table, weights_in, wave_in, right_mine, right_sib, left_mine, below, above,
    first, last, carried_out, correlation,
    weights, result, carried, wave, right, left, sems, carried_sems,
):
    blocks = wave.shape[0]
    most = last.shape[0]
    first_slots = blocks - most
    copies = [
        pltpu.make_async_copy(source, target, sems.at[n])
        for n, (source, target) in enumerate(
            (
                (wave_in, wave),
                (right_mine, right.at[0]),
                (right_sib, right.at[1]),
                (weights_in, weights),
                (left_mine, left.at[0]),
                (below, left.at[1]),
                (above, left.at[2]),
            )
        )
    ]
    for copy in copies:
        copy.start()
    result[...] = jnp.zeros_like(result)
    correlation[...] = jnp.zeros_like(correlation)
    skipped = count_of(table, 0, blocks, -1)
    end = blocks - count_of(table, 0, blocks, 3)
    for copy in copies[:4]:
        copy.wait()

    def carry(slot):
        return carried_of(
            wave[table[slot, 1]], right[table[slot, 3], :, table[slot, 4]], weights[pl.ds(table[slot, 5], 1), :]
        )

    def written(slot):
        at = slot - first_slots
        return pltpu.make_async_copy(carried.at[at], carried_out.at[at], carried_sems.at[at])

    def keep(slot, _):
        carried[slot - first_slots] = carry(slot)

    grouped(end, blocks, 4, keep)

    @pl.loop(end, blocks)
    def _(slot):
        written(slot).start()

    for copy in copies[4:]:
        copy.wait()

    def apply(slot, counted):
        found = applied(left[table[slot, 0], :, table[slot, 2]], carry(slot))
        result[slot] = found.astype(result.dtype)
        correlation[...] += paired(found, wave[table[slot, 1]], counted)

    grouped(skipped, end, 4, apply)
    outs = [
        pltpu.make_async_copy(result.at[part], target, sems.at[len(copies) + n])
        for n, (part, target) in enumerate(
            ((pl.ds(0, first_slots), first), (pl.ds(first_slots, most), last))
        )
    ]
    for out in outs:
        out.start()
    for out in outs:
        out.wait()

    @pl.loop(end, blocks)
    def _(slot):
        written(slot).wait()


def guest_kernel(
    flags, table, weights_in, below, above, wave_own, wave_other, right_mine, right_sib,
    own_out, other_out, correlation,
    weights, wave, right, left, sems,
):
    half = own_out.shape[0]
    counts = [count_of(table, part * half, half, 3) for part in range(2)]
    copies = [
        pltpu.make_async_copy(source, target, sems.at[n])
        for n, (source, target) in enumerate(
            (
                (right_mine, right.at[0]),
                (right_sib, right.at[1]),
                (wave_own.at[pl.ds(0, half)], wave.at[pl.ds(0, half)]),
                (wave_other.at[pl.ds(0, half)], wave.at[pl.ds(half, half)]),
                (weights_in, weights),
            )
        )
    ]

    @pl.when(counts[0] + counts[1] > 0)
    def _():
        for copy in copies:
            copy.start()
        choose(flags[0] == 1, above, below, left, sems.at[len(copies)])

    own_out[...] = jnp.zeros_like(own_out)
    other_out[...] = jnp.zeros_like(other_out)
    correlation[...] = jnp.zeros_like(correlation)

    @pl.when(counts[0] + counts[1] > 0)
    def _():
        for copy in copies:
            copy.wait()
        pltpu.make_async_copy(above, left, sems.at[len(copies)]).wait()

    for part, target in enumerate((own_out, other_out)):

        def apply(row, counted):
            carried = carried_of(
                wave[row],
                right[flags[1 + part], :, table[row, 4]],
                weights[pl.ds(table[row, 5], 1), :],
            )
            result = applied(left[:, table[row, 2]], carried)
            target[row - part * half] = result.astype(target.dtype)
            correlation[...] += paired(result, wave[row], counted)

        grouped(part * half, part * half + counts[part], 4, apply)


def far_kernel(
    flags, table, carried_own, carried_other, below, above, own, other, wave_own, wave_other,
    own_out, other_out, correlation,
    held, wave, left, sems, wave_sems, more_sems,
):
    half = own_out.shape[0]
    lows = [half - count_of(table, part * half, half, 3) for part in range(2)]
    choose(flags[0] == 1, above, below, left, more_sems.at[0])
    kept = [
        pltpu.make_async_copy(source, target, more_sems.at[1 + n])
        for n, (source, target) in enumerate(((own, own_out), (other, other_out)))
    ]
    for copy in kept:
        copy.start()
    for part, (carried, waves) in enumerate(((carried_own, wave_own), (carried_other, wave_other))):

        @pl.loop(lows[part], half)
        def _(slot):
            row = part * half + slot
            pltpu.make_async_copy(carried.at[slot], held.at[row], sems.at[row]).start()
            pltpu.make_async_copy(waves.at[table[row, 1]], wave.at[row], wave_sems.at[row]).start()

    correlation[...] = jnp.zeros_like(correlation)
    for copy in kept:
        copy.wait()
    pltpu.make_async_copy(above, left, more_sems.at[0]).wait()
    for part, (carried, target) in enumerate(((carried_other, other_out), (carried_own, own_out))):
        part = 1 - part

        @pl.loop(lows[part], half)
        def _(slot):
            row = part * half + slot
            pltpu.make_async_copy(carried.at[slot], held.at[row], sems.at[row]).wait()
            pltpu.make_async_copy(wave_own.at[0], wave.at[row], wave_sems.at[row]).wait()

        def apply(slot, counted):
            row = part * half + slot
            result = applied(left[:, table[row, 2]], held[row])
            target[slot] = result.astype(target.dtype)
            correlation[...] += paired(result, wave[row], counted)

        grouped(lows[part], half, 4, apply)


def pick_kernel(table, own, facts, out):
    slots = out.shape[0] - 1
    out[slots] = facts[0]

    @pl.loop(0, slots)
    def _(slot):
        out[slot] = own[table[slot, 1]]


def first_kernel(table, own, got, wave, whole, sums):
    blocks = wave.shape[0]
    zero = jnp.zeros((8, 128), jnp.float32)
    whole[...] = own[...] + got[...].astype(jnp.float32)
    count = count_of(table, 0, blocks, 1)

    def add(n, totals):
        value, found = wave[table[n, 1]].astype(jnp.float32), whole[table[n, 2]]
        return totals[0] + folded(value * value), totals[1] + folded(value * found)

    norm_map, correlation_map = lax.fori_loop(0, count, add, (zero, zero))
    norm = jnp.sum(norm_map, keepdims=True)
    correlation = jnp.sum(correlation_map, keepdims=True)
    ratio = ratio_of(norm, correlation)

    def rest(n, total):
        residual = whole[table[n, 2]] - ratio * wave[table[n, 1]].astype(jnp.float32)
        return total + folded(residual * residual)

    resid = jnp.sum(lax.fori_loop(0, count, rest, zero), keepdims=True)
    sums[...] = lined(norm, correlation, resid)


def lined(*values):
    line = lax.broadcasted_iota(jnp.int32, (8, 128), 0)
    result = jnp.zeros((8, 128), jnp.float32)
    for n, value in enumerate(values):
        result = jnp.where(line == n, value, result)
    return result


def sum_kernel(one, two, out):
    out[...] = one[...].astype(out.dtype) + two[...].astype(out.dtype)


def late_kernel(
    table, sums_first, last_own, last_got, guest_full, wave, map_a, map_b, map_c, map_d, late, sums
):
    blocks = wave.shape[0]
    most = last_own.shape[0]
    zero = jnp.zeros((8, 128), jnp.float32)
    late[pl.ds(0, most)] = last_own[...] + last_got[...].astype(jnp.float32)
    late[pl.ds(most, most)] = guest_full[...]
    count = count_of(table, 0, blocks, 1)

    def add(n, totals):
        value, found = wave[table[n, 1]].astype(jnp.float32), late[table[n, 2]]
        return totals[0] + folded(value * value), totals[1] + folded(value * found)

    norm_map, correlation_map = lax.fori_loop(0, count, add, (zero, zero))
    norm = jnp.sum(norm_map, keepdims=True)
    correlation = jnp.sum(correlation_map, keepdims=True)
    ratio = ratio_of(norm, correlation)

    def rest(n, total):
        residual = late[table[n, 2]] - ratio * wave[table[n, 1]].astype(jnp.float32)
        return total + folded(residual * residual)

    resid = jnp.sum(lax.fori_loop(0, count, rest, zero), keepdims=True)
    first = [sums_first[n : n + 1, 0:1] for n in range(4)]
    exact = jnp.sum(map_a[...] + map_b[...] + map_c[...] + map_d[...], keepdims=True)
    sums[...] = lined(*merged(first, (norm, correlation, resid, exact)))


def place_kernel(table, first_own, late_own, first_sib, late_sib, kept):
    @pl.loop(0, kept.shape[0])
    def _(k):
        for code, source in enumerate((first_own, late_own, first_sib, late_sib)):

            @pl.when(table[k, 0] == code)
            def _():
                kept[k] = source[table[k, 1]]


def correction_kernel(
    entries, sums, near, far, across, image, wave, image_out, out, ratio, result, sems
):
    chunks = sems.shape[0] - 1
    size = image.shape[0] // chunks

    def total(ref):
        parts = [[ref[base + n : base + n + 1, 0:1] for n in range(4)] for base in (0, 8, 16, 24)]
        return merged(merged(*parts[:2]), merged(*parts[2:]))

    whole = merged(merged(total(sums), total(near)), merged(total(far), total(across)))
    rayleigh = whole[3] / whole[0]
    gap = ratio_of(whole[0], whole[1]) - rayleigh
    scale = lax.rsqrt((whole[2] + gap * gap * whole[0]) / entries + 1e-06)
    ratio[0] = rayleigh[0, 0]
    copies = [pltpu.make_async_copy(image, image_out, sems.at[chunks])]
    copies[0].start()
    for n in range(chunks):
        part = pl.ds(n * size, size)
        result[part] = (image[part] - rayleigh * wave[part].astype(jnp.float32)) * scale
        copies.append(pltpu.make_async_copy(result.at[part], out.at[part], sems.at[n]))
        copies[-1].start()
    for copy in copies:
        copy.wait()


def ratio_of(norm, correlation):
    return jnp.where(norm > 0, correlation / jnp.where(norm > 0, norm, 1.0), 0.0)


def merged(one, two):
    low, high = jnp.minimum(one[0], two[0]), jnp.maximum(one[0], two[0])
    norm = one[0] + two[0]
    gap = ratio_of(one[0], one[1]) - ratio_of(two[0], two[1])
    shared = low * jnp.where(norm > 0, high / jnp.where(norm > 0, norm, 1.0), 0.0)
    return norm, one[1] + two[1], one[2] + two[2] + gap * gap * shared, one[3] + two[3]


def ranks(key):
    at = jnp.arange(key.shape[-1])
    mine, others = key[..., :, None], key[..., None, :]
    before = (others < mine) | ((others == mine) & (at[None, :] < at[:, None]))
    return jnp.sum(before.astype(jnp.int32), axis=-1)


def call(kernel, out_shape, in_spaces, out_spaces, scratch, flops=1, aliases={}, vmem=VMEM_LIMIT):
    return pl.pallas_call(
        kernel,
        out_shape=out_shape,
        in_specs=[pl.BlockSpec(memory_space=space) for space in in_spaces],
        out_specs=jax.tree.map(lambda space: pl.BlockSpec(memory_space=space), out_spaces),
        scratch_shapes=scratch,
        input_output_aliases=aliases,
        compiler_params=pltpu.CompilerParams(vmem_limit_bytes=vmem),
        cost_estimate=pl.CostEstimate(
            flops=flops, bytes_accessed=1, transcendentals=0
        ),
    )


def after(array, *others):
    return lax.optimization_barrier((array, *others))[0]


def on_device(
    wavefunction,
    left_sector,
    right_sector,
    phys_index,
    left_environment,
    right_environment,
    term_weights,
):
    blocks, dim, _ = wavefunction.shape
    terms, per_device = left_environment.shape[:2]
    most = 2 * max(1, blocks // 8)
    first_slots = blocks - most
    index = lax.axis_index("sector")
    z, y, c = index // 2, index % 2, lax.axis_index("term")
    flags = jnp.stack([z < 2, y != c, y == c]).astype(jnp.int32)

    def hop(array, step, where=lambda z, y, c: True):
        return move(array, pairs_of(step, where))

    def mine_of(own, swapped):
        return jnp.where(y == c, own, swapped)

    def tiled(facts):
        rows, columns = facts.shape
        return jnp.pad(facts.astype(bf16), ((0, dim - rows), (0, dim - columns)))[None]

    HBM, VMEM, SMEM = pltpu.HBM, pltpu.VMEM, pltpu.SMEM
    bf16, f32 = jnp.bfloat16, jnp.float32
    square = (dim, dim)
    env = (terms, per_device) + square
    info = jnp.stack([left_sector, right_sector - index * per_device, phys_index])
    parity = jnp.stack([c, c, 1 - c])[:, None]
    side = jnp.where(jnp.arange(2) == 0, y, 1 - y)

    def sorted_out(infos, count):
        left_device = infos[:, 0] // per_device
        step = left_device // 2 - z
        stage = jnp.where(step == 0, 0, jnp.where(step == -1, 1, jnp.where(step == 1, 2, 3)))
        here = left_device % 2 == parity[:count]
        guest = here & (jnp.abs(step) == 3)
        stage = jnp.where(here & ~guest, stage, -1)
        place = ranks(jnp.where(stage < 0, 0, jnp.where(stage == 3, 2, 1)))
        return here, guest, stage, place

    def ordered(places, rows, fields):
        chosen = (jnp.arange(rows)[None, :, None] == places[:, None, :]).astype(f32)
        values = jnp.stack(fields, axis=-1).astype(f32)
        return jnp.einsum("rsk,rkf->rsf", chosen, values, precision=lax.Precision.HIGHEST).astype(
            jnp.int32
        )

    weights_sib = move(term_weights, CORE)
    left_n = move(left_environment, DIAGONAL)
    left_n, weights_sib = lax.optimization_barrier((left_n, weights_sib))
    weights = mine_of(term_weights, weights_sib).astype(f32).T
    weights = jnp.broadcast_to(weights[:, :, None], weights.shape + (dim,)).reshape(-1, terms * dim)
    left_mine = mine_of(left_environment, left_n)
    below = hop(left_mine, up)
    above = hop(left_mine, down)

    right_n = move(after(right_environment, left_mine), DIAGONAL)
    right_mine = mine_of(right_environment, right_n)
    info_other = move(after(info, left_mine), COLUMN)

    block = jnp.arange(blocks)
    _, guest, _, _ = sorted_out(info[None], 1)
    guest_place = ranks(jnp.where(guest, 0, 1))
    guest_fields = [jnp.where(guest, 3, -1), block[None], info[None, 0] % per_device]
    guest_fields += [jnp.broadcast_to(side[:1, None] != c, (1, blocks)), info[None, 1], info[None, 2]]
    guest_table = ordered(guest_place, most, guest_fields)[0]
    picked = call(
        pick_kernel,
        jax.ShapeDtypeStruct((most + 1,) + square, bf16),
        [SMEM, VMEM, VMEM],
        VMEM,
        [],
    )(guest_table, after(wavefunction, info_other), tiled(guest_table))
    wave_guest = move(after(picked, left_mine), GUEST)

    infos = jnp.stack([info, info_other, info])
    here, guest, stage, place = sorted_out(infos, 3)
    guest_place = ranks(jnp.where(guest, 0, 1))
    table = ordered(
        place[:2],
        blocks,
        [
            stage[:2],
            jnp.broadcast_to(block, (2, blocks)),
            infos[:2, 0] % per_device,
            jnp.broadcast_to(side[:, None] != c, (2, blocks)),
            infos[:2, 1],
            infos[:2, 2],
        ],
    )
    far_table = table[:, first_slots:].reshape(2 * most, -1)
    table = table.reshape(2 * blocks, -1)
    table = table.reshape(2, blocks, -1)

    def source_of(which, of):
        late_place = jnp.where(guest[of], most + guest_place[of], place[of] - first_slots)
        late = guest[of] | (place[of] >= first_slots)
        return jnp.stack(
            [2 * which + late.astype(jnp.int32), jnp.where(late, late_place, place[of])], axis=-1
        )

    sources = jnp.where(here[0][:, None], source_of(0, 0), source_of(1, 2))
    picked_out = jnp.stack([sources[:, 0] == 0, sources[:, 0] == 1]).astype(jnp.int32)
    first_table, late_table = ordered(
        ranks(1 - picked_out),
        blocks,
        [
            picked_out,
            jnp.broadcast_to(block, (2, blocks)),
            jnp.broadcast_to(sources[:, 1], (2, blocks)),
        ],
    )

    held = (below, above, right_mine, wave_guest)
    held += (table, far_table, weights, sources, first_table, late_table)
    held = lax.optimization_barrier(held)
    below, above, right_mine, wave_guest = held[:4]
    table, far_table, weights, sources, first_table, late_table = held[4:]
    below_two = hop(below, up, inner)
    above_two = hop(above, down, inner)
    right_guest = hop(right_mine, inward, outer)
    wave_other = move(after(wavefunction, right_mine), COLUMN)
    right_sib = move(right_mine, CORE)
    map_shape = jax.ShapeDtypeStruct((8, 128), f32)

    def near(relation, blocks_of, kind):
        return call(
            near_kernel,
            (
                jax.ShapeDtypeStruct((first_slots,) + square, kind),
                jax.ShapeDtypeStruct((most,) + square, kind),
                jax.ShapeDtypeStruct((most, dim, terms * dim), bf16),
                map_shape,
            ),
            [SMEM] + [HBM] * 7,
            (HBM, HBM, HBM, VMEM),
            [
                pltpu.VMEM(weights.shape, f32),
                pltpu.VMEM((blocks,) + square, kind),
                pltpu.VMEM((most, dim, terms * dim), bf16),
                pltpu.VMEM((blocks,) + square, bf16),
                pltpu.VMEM((2,) + env, bf16),
                pltpu.VMEM((3,) + env, bf16),
                pltpu.SemaphoreType.DMA((9,)),
                pltpu.SemaphoreType.DMA((most,)),
            ],
        )(
            table[relation], weights, blocks_of, right_mine, right_sib,
            left_mine, below, above,
        )

    own, own_last, carried_own, map_own = near(0, wavefunction, f32)
    other, other_last, carried_other, map_other = near(1, wave_other, bf16)
    wave_guest_other = move(after(wave_guest, own), COLUMN_INNER)
    held = (below_two, above_two, right_guest, wave_guest_other)
    held += (own, own_last, carried_own, other, other_last, carried_other)
    held = lax.optimization_barrier(held)
    below_two, above_two, right_guest, wave_guest_other = held[:4]
    own, own_last, carried_own, other, other_last, carried_other = held[4:]
    first_got = move(other, COLUMN)
    right_guest_sib = hop(right_guest, other_core, inner)
    guest_got = jnp.concatenate(
        [guests[most, :most, :6] for guests in (wave_guest, wave_guest_other)]
    ).astype(jnp.int32)

    last = jax.ShapeDtypeStruct((most,) + square, f32)
    last_sent = jax.ShapeDtypeStruct((most,) + square, bf16)
    guest_own, guest_other, map_guest = call(
        guest_kernel,
        (last_sent, last_sent, map_shape),
        [SMEM] * 2 + [HBM] * 7,
        (VMEM,) * 3,
        [
            pltpu.VMEM(weights.shape, f32),
            pltpu.VMEM((2 * most,) + square, bf16),
            pltpu.VMEM((2,) + env, bf16),
            pltpu.VMEM(env, bf16),
            pltpu.SemaphoreType.DMA((6,)),
        ],
        vmem=VMEM_SMALL,
    )(
        flags, guest_got, weights, below_two, above_two,
        wave_guest, wave_guest_other, right_guest, right_guest_sib,
    )
    guest_straight = move(guest_own, GUEST_BACK)
    guest_crossed = move(guest_other, GUEST_BACK_CROSSED)
    last_own, last_other, map_far = call(
        far_kernel,
        (last, last_sent, map_shape),
        [SMEM] * 2 + [HBM] * 8,
        (VMEM,) * 3,
        [
            pltpu.VMEM((2 * most, dim, terms * dim), bf16),
            pltpu.VMEM((2 * most,) + square, bf16),
            pltpu.VMEM(env, bf16),
            pltpu.SemaphoreType.DMA((2 * most,)),
            pltpu.SemaphoreType.DMA((2 * most,)),
            pltpu.SemaphoreType.DMA((3,)),
        ],
        2**37,
    )(
        flags, after(far_table, guest_own), carried_own, carried_other, below_two, above_two,
        own_last, other_last, wavefunction, wave_other,
    )
    last_got = move(last_other, COLUMN)
    first_own, sums_first = call(
        first_kernel,
        (jax.ShapeDtypeStruct((first_slots,) + square, f32), jax.ShapeDtypeStruct((8, 128), f32)),
        [SMEM] + [VMEM] * 3,
        (VMEM, VMEM),
        [],
        vmem=VMEM_SMALL,
    )(first_table, own, after(first_got, last_own), wavefunction)
    first_sib = move(first_own, CORE)
    guest_full = call(sum_kernel, last, [VMEM] * 2, VMEM, [], 2**37, vmem=VMEM_SMALL)(
        after(guest_straight, sums_first), guest_crossed
    )
    late, sums = call(
        late_kernel,
        (jax.ShapeDtypeStruct((2 * most,) + square, f32), jax.ShapeDtypeStruct((8, 128), f32)),
        [SMEM] + [VMEM] * 9,
        (VMEM, VMEM),
        [],
        vmem=VMEM_SMALL,
    )(
        late_table, sums_first, last_own, last_got, guest_full, wavefunction,
        map_own, map_other, map_guest, map_far,
    )
    late_sib = move(late, CORE)
    image_shape = jax.ShapeDtypeStruct((blocks,) + square, f32)
    kept = call(
        place_kernel,
        image_shape,
        [SMEM] + [VMEM] * 4,
        VMEM,
        [],
        vmem=VMEM_SMALL,
    )(sources, first_own, late, first_sib, late_sib)
    sums = jnp.concatenate([sums] + [move(sums, pairs) for pairs in (CORE, COLUMN, ACROSS)])
    sums = [sums] + [move(sums, pairs_of(lambda z, y, c: (z ^ n, y, c))) for n in (1, 2, 3)]
    image, correction, rayleigh = call(
        functools.partial(correction_kernel, blocks * 8 * dim * dim),
        (image_shape, image_shape, jax.ShapeDtypeStruct((1,), f32)),
        [VMEM] * 6,
        (HBM, HBM, SMEM),
        [pltpu.VMEM((blocks,) + square, f32), pltpu.SemaphoreType.DMA((9,))],
        vmem=VMEM_SMALL,
    )(*sums, kept, wavefunction)
    return image, correction, rayleigh


def solution(mesh):
    placed = (
        P(("parts", "sector"), None, None),
        P(("parts", "sector")),
        P(("parts", "sector")),
        P(("parts", "sector")),
        P(("parts", "term"), "sector", None, None),
        P(("parts", "term"), "sector", None, None),
        P(("parts", "term"), None),
    )
    paired = mesh.shape["sector"] == 8 and mesh.shape["term"] == 2
    return jax.shard_map(
        on_device if paired else on_device_any,
        mesh=mesh,
        in_specs=placed,
        out_specs=(
            P(("parts", "sector"), None, None),
            P(("parts", "sector"), None, None),
            P("parts"),
        ),
        check_vma=False,
    )
```

```python
import functools

import jax
import jax.numpy as jnp
from jax import lax
from jax.experimental import pallas as pl
from jax.experimental.pallas import tpu as pltpu
from jax.sharding import PartitionSpec as P

BOTH = ("sector", "term")
VMEM_LIMIT = 60 * 2**20
VMEM_SMALL = 32 * 2**20


def on_device_any(
    wavefunction,
    left_sector,
    right_sector,
    phys_index,
    left_environment,
    right_environment,
    term_weights,
):
    blocks = wavefunction.shape[0]
    sector_dim = wavefunction.shape[1]
    sector_count = lax.axis_size("sector")
    per_device = right_environment.shape[1]
    capacity = 2 * max(1, blocks // sector_count)
    own_index = lax.axis_index("sector")
    right_local = right_sector - own_index * per_device
    target = left_sector // per_device
    positions = jnp.arange(blocks)
    earlier = (target[None, :] == target[:, None]) & (positions[None, :] < positions[:, None])
    placement_order = jnp.sum(earlier.astype(jnp.int32), axis=1)
    physical_selector_matrix = (
        phys_index[:, None] == jnp.arange(term_weights.shape[1])[None, :]
    ).astype(jnp.bfloat16)
    slot_index = target * capacity + placement_order
    slot_count = sector_count * capacity
    selector_f = (jnp.arange(slot_count)[:, None] == slot_index[None, :]).astype(jnp.float32)
    wanted = jnp.dot(
        selector_f, (left_sector % per_device).astype(jnp.float32), precision=lax.Precision.HIGHEST
    ).astype(jnp.int32)
    requests = lax.all_to_all(
        wanted.reshape(sector_count, capacity), "sector", split_axis=0, concat_axis=0, tiled=True
    )
    picked = jnp.take(left_environment, requests.reshape(-1), axis=1)
    picked = jnp.moveaxis(picked, 0, 1).reshape(
        sector_count, capacity, left_environment.shape[0], sector_dim, sector_dim
    )
    fetched = lax.all_to_all(picked, "sector", split_axis=0, concat_axis=0, tiled=True)
    left_blocks = jnp.take(
        fetched.reshape(slot_count, left_environment.shape[0], sector_dim, sector_dim),
        slot_index,
        axis=0,
    )
    right_taken = jnp.take(right_environment, right_local, axis=1)
    block_weights = jnp.dot(
        physical_selector_matrix, term_weights.T, preferred_element_type=jnp.float32
    )
    environment_product = jnp.einsum(
        "kab,tkcb->ktac", wavefunction, right_taken, preferred_element_type=jnp.float32
    )
    carried = (environment_product * block_weights[:, :, None, None]).astype(jnp.bfloat16)
    image_partial_result = jnp.einsum(
        "ktij,ktjc->kic", left_blocks, carried, preferred_element_type=jnp.float32
    )
    image = lax.psum(image_partial_result, "term")
    wave_f32 = wavefunction.astype(jnp.float32)
    norm_wave = jnp.sum(wave_f32 * wave_f32)
    correlation = jnp.sum(wave_f32 * image)
    entries = blocks * sector_count * sector_dim * sector_dim
    norm_all, correlation_all = lax.psum((norm_wave, correlation), "sector")
    rayleigh = correlation_all / norm_all
    residual = image - rayleigh * wave_f32
    norm_resid = lax.psum(jnp.sum(residual * residual), "sector")
    correction = residual * lax.rsqrt(norm_resid / entries + 1e-06)
    return (image, correction, jnp.reshape(rayleigh, (1,)))


def pairs_of(target, chosen=lambda z, y, c: True):
    found = []
    for z in range(4):
        for y in range(2):
            for c in range(2):
                if chosen(z, y, c):
                    to = target(z, y, c)
                    if 0 <= to[0] < 4:
                        found.append(((z * 2 + y) * 2 + c, (to[0] * 2 + to[1]) * 2 + to[2]))
    return found


def inner(z, y, c):
    return z in (1, 2)


def outer(z, y, c):
    return z in (0, 3)


def straight(z, y, c):
    return y == c


def crossed(z, y, c):
    return y != c


def both(one, two):
    return lambda z, y, c: one(z, y, c) and two(z, y, c)


def up(z, y, c):
    return z + 1, y, c


def down(z, y, c):
    return z - 1, y, c


def other_core(z, y, c):
    return z, y, 1 - c


def other_column(z, y, c):
    return z, 1 - y, c


def inward(z, y, c):
    return (1 if z == 0 else 2), y, c


def outward(z, y, c):
    return (0 if z == 1 else 3), y, c


def outward_crossed(z, y, c):
    return (0 if z == 1 else 3), 1 - y, c


DIAGONAL = pairs_of(lambda z, y, c: (z, 1 - y, 1 - c), crossed)
CORE = pairs_of(other_core)
COLUMN = pairs_of(other_column)
ACROSS = pairs_of(lambda z, y, c: (z, 1 - y, 1 - c))
COLUMN_INNER = pairs_of(other_column, inner)
GUEST = pairs_of(inward, outer)
GUEST_BACK = pairs_of(outward, inner)
GUEST_BACK_CROSSED = pairs_of(outward_crossed, inner)


def move(array, pairs):
    return lax.ppermute(array, BOTH, pairs)


def carried_of(wave, right, weights):
    terms, dim, _ = right.shape
    product = lax.dot_general(
        wave,
        right.reshape(terms * dim, dim),
        (((1,), (1,)), ((), ())),
        preferred_element_type=jnp.float32,
    )
    return (product * weights).astype(jnp.bfloat16)


def applied(left, carried):
    terms, dim, _ = left.shape
    lefts = jnp.concatenate([left[t] for t in range(terms)], axis=1)
    stacked = jnp.concatenate(
        [carried[:, t * dim : (t + 1) * dim] for t in range(terms)], axis=0
    )
    return jnp.dot(lefts, stacked, preferred_element_type=jnp.float32)


def choose(flag, one, two, target, sem):
    @pl.when(flag)
    def _():
        pltpu.make_async_copy(one, target, sem).start()

    @pl.when(jnp.logical_not(flag))
    def _():
        pltpu.make_async_copy(two, target, sem).start()


def grouped(low, high, step, body):
    @pl.loop(0, (high - low + step - 1) // step)
    def _(group):
        for n in range(step):
            row = low + group * step + n
            body(jnp.minimum(row, high - 1), (row < high).astype(jnp.float32))


def folded(value):
    return jnp.sum(value.reshape(-1, 8, 128), axis=0)


def paired(found, wave, counted):
    return folded(found * wave.astype(jnp.float32)) * counted


def count_of(table, base, rows, stage):
    def add(row, total):
        return total + (table[base + row, 0] == stage).astype(jnp.int32)

    return lax.fori_loop(0, rows, add, jnp.int32(0))


def select_kernel(flags, straight_side, crossed_side, out, held, sems):
    terms = held.shape[0]
    outs = [pltpu.make_async_copy(held.at[t], out.at[t], sems.at[1, t]) for t in range(terms)]
    for t in range(terms):
        choose(flags[2] == 1, straight_side.at[t], crossed_side.at[t], held.at[t], sems.at[0, t])
    for t in range(terms):
        pltpu.make_async_copy(straight_side.at[t], held.at[t], sems.at[0, t]).wait()
        outs[t].start()
    for t in range(terms):
        outs[t].wait()


def near_kernel(
    table, weights_in, wave_in, right_mine, right_sib, left_mine, below, above,
    first, last, carried_out, correlation,
    weights, result, carried, wave, right, left, sems, carried_sems,
):
    blocks = wave.shape[0]
    most = last.shape[0]
    first_slots = blocks - most
    copies = [
        pltpu.make_async_copy(source, target, sems.at[n])
        for n, (source, target) in enumerate(
            (
                (wave_in, wave),
                (right_mine, right.at[0]),
                (right_sib, right.at[1]),
                (weights_in, weights),
                (left_mine, left.at[0]),
                (below, left.at[1]),
                (above, left.at[2]),
            )
        )
    ]
    for copy in copies:
        copy.start()
    result[...] = jnp.zeros_like(result)
    correlation[...] = jnp.zeros_like(correlation)
    skipped = count_of(table, 0, blocks, -1)
    end = blocks - count_of(table, 0, blocks, 3)
    for copy in copies[:4]:
        copy.wait()

    def carry(slot):
        return carried_of(
            wave[table[slot, 1]], right[table[slot, 3], :, table[slot, 4]], weights[pl.ds(table[slot, 5], 1), :]
        )

    def written(slot):
        at = slot - first_slots
        return pltpu.make_async_copy(carried.at[at], carried_out.at[at], carried_sems.at[at])

    def keep(slot, _):
        carried[slot - first_slots] = carry(slot)

    grouped(end, blocks, 4, keep)

    @pl.loop(end, blocks)
    def _(slot):
        written(slot).start()

    for copy in copies[4:]:
        copy.wait()

    def apply(slot, counted):
        found = applied(left[table[slot, 0], :, table[slot, 2]], carry(slot))
        result[slot] = found.astype(result.dtype)
        correlation[...] += paired(found, wave[table[slot, 1]], counted)

    grouped(skipped, end, 4, apply)
    outs = [
        pltpu.make_async_copy(result.at[part], target, sems.at[len(copies) + n])
        for n, (part, target) in enumerate(
            ((pl.ds(0, first_slots), first), (pl.ds(first_slots, most), last))
        )
    ]
    for out in outs:
        out.start()
    for out in outs:
        out.wait()

    @pl.loop(end, blocks)
    def _(slot):
        written(slot).wait()


def guest_kernel(
    flags, table, weights_in, below, above, wave_own, wave_other, right_mine, right_sib,
    own_out, other_out, correlation,
    weights, wave, right, left, sems,
):
    half = own_out.shape[0]
    counts = [count_of(table, part * half, half, 3) for part in range(2)]
    copies = [
        pltpu.make_async_copy(source, target, sems.at[n])
        for n, (source, target) in enumerate(
            (
                (right_mine, right.at[0]),
                (right_sib, right.at[1]),
                (wave_own.at[pl.ds(0, half)], wave.at[pl.ds(0, half)]),
                (wave_other.at[pl.ds(0, half)], wave.at[pl.ds(half, half)]),
                (weights_in, weights),
            )
        )
    ]

    @pl.when(counts[0] + counts[1] > 0)
    def _():
        for copy in copies:
            copy.start()
        choose(flags[0] == 1, above, below, left, sems.at[len(copies)])

    own_out[...] = jnp.zeros_like(own_out)
    other_out[...] = jnp.zeros_like(other_out)
    correlation[...] = jnp.zeros_like(correlation)

    @pl.when(counts[0] + counts[1] > 0)
    def _():
        for copy in copies:
            copy.wait()
        pltpu.make_async_copy(above, left, sems.at[len(copies)]).wait()

    for part, target in enumerate((own_out, other_out)):

        def apply(row, counted):
            carried = carried_of(
                wave[row],
                right[flags[1 + part], :, table[row, 4]],
                weights[pl.ds(table[row, 5], 1), :],
            )
            result = applied(left[:, table[row, 2]], carried)
            target[row - part * half] = result.astype(target.dtype)
            correlation[...] += paired(result, wave[row], counted)

        grouped(part * half, part * half + counts[part], 4, apply)


def far_kernel(
    flags, table, carried_own, carried_other, below, above, own, other, wave_own, wave_other,
    own_out, other_out, correlation,
    held, wave, left, sems, wave_sems, more_sems,
):
    half = own_out.shape[0]
    lows = [half - count_of(table, part * half, half, 3) for part in range(2)]
    choose(flags[0] == 1, above, below, left, more_sems.at[0])
    kept = [
        pltpu.make_async_copy(source, target, more_sems.at[1 + n])
        for n, (source, target) in enumerate(((own, own_out), (other, other_out)))
    ]
    for copy in kept:
        copy.start()
    for part, (carried, waves) in enumerate(((carried_own, wave_own), (carried_other, wave_other))):

        @pl.loop(lows[part], half)
        def _(slot):
            row = part * half + slot
            pltpu.make_async_copy(carried.at[slot], held.at[row], sems.at[row]).start()
            pltpu.make_async_copy(waves.at[table[row, 1]], wave.at[row], wave_sems.at[row]).start()

    correlation[...] = jnp.zeros_like(correlation)
    for copy in kept:
        copy.wait()
    pltpu.make_async_copy(above, left, more_sems.at[0]).wait()
    for part, (carried, target) in enumerate(((carried_other, other_out), (carried_own, own_out))):
        part = 1 - part

        @pl.loop(lows[part], half)
        def _(slot):
            row = part * half + slot
            pltpu.make_async_copy(carried.at[slot], held.at[row], sems.at[row]).wait()
            pltpu.make_async_copy(wave_own.at[0], wave.at[row], wave_sems.at[row]).wait()

        def apply(slot, counted):
            row = part * half + slot
            result = applied(left[:, table[row, 2]], held[row])
            target[slot] = result.astype(target.dtype)
            correlation[...] += paired(result, wave[row], counted)

        grouped(lows[part], half, 4, apply)


def pick_kernel(table, own, facts, out):
    slots = out.shape[0] - 1
    out[slots] = facts[0]

    @pl.loop(0, slots)
    def _(slot):
        out[slot] = own[table[slot, 1]]


def first_kernel(table, own, got, wave, whole, sums):
    blocks = wave.shape[0]
    zero = jnp.zeros((8, 128), jnp.float32)
    whole[...] = own[...] + got[...].astype(jnp.float32)
    count = count_of(table, 0, blocks, 1)

    def add(n, totals):
        value, found = wave[table[n, 1]].astype(jnp.float32), whole[table[n, 2]]
        return totals[0] + folded(value * value), totals[1] + folded(value * found)

    norm_map, correlation_map = lax.fori_loop(0, count, add, (zero, zero))
    norm = jnp.sum(norm_map, keepdims=True)
    correlation = jnp.sum(correlation_map, keepdims=True)
    ratio = ratio_of(norm, correlation)

    def rest(n, total):
        residual = whole[table[n, 2]] - ratio * wave[table[n, 1]].astype(jnp.float32)
        return total + folded(residual * residual)

    resid = jnp.sum(lax.fori_loop(0, count, rest, zero), keepdims=True)
    sums[...] = lined(norm, correlation, resid)


def lined(*values):
    line = lax.broadcasted_iota(jnp.int32, (8, 128), 0)
    result = jnp.zeros((8, 128), jnp.float32)
    for n, value in enumerate(values):
        result = jnp.where(line == n, value, result)
    return result


def sum_kernel(one, two, out):
    out[...] = one[...].astype(out.dtype) + two[...].astype(out.dtype)


def late_kernel(
    table, sums_first, last_own, last_got, guest_full, wave, map_a, map_b, map_c, map_d, late, sums
):
    blocks = wave.shape[0]
    most = last_own.shape[0]
    zero = jnp.zeros((8, 128), jnp.float32)
    late[pl.ds(0, most)] = last_own[...] + last_got[...].astype(jnp.float32)
    late[pl.ds(most, most)] = guest_full[...]
    count = count_of(table, 0, blocks, 1)

    def add(n, totals):
        value, found = wave[table[n, 1]].astype(jnp.float32), late[table[n, 2]]
        return totals[0] + folded(value * value), totals[1] + folded(value * found)

    norm_map, correlation_map = lax.fori_loop(0, count, add, (zero, zero))
    norm = jnp.sum(norm_map, keepdims=True)
    correlation = jnp.sum(correlation_map, keepdims=True)
    ratio = ratio_of(norm, correlation)

    def rest(n, total):
        residual = late[table[n, 2]] - ratio * wave[table[n, 1]].astype(jnp.float32)
        return total + folded(residual * residual)

    resid = jnp.sum(lax.fori_loop(0, count, rest, zero), keepdims=True)
    first = [sums_first[n : n + 1, 0:1] for n in range(4)]
    exact = jnp.sum(map_a[...] + map_b[...] + map_c[...] + map_d[...], keepdims=True)
    sums[...] = lined(*merged(first, (norm, correlation, resid, exact)))


def place_kernel(table, first_own, late_own, first_sib, late_sib, kept):
    @pl.loop(0, kept.shape[0])
    def _(k):
        for code, source in enumerate((first_own, late_own, first_sib, late_sib)):

            @pl.when(table[k, 0] == code)
            def _():
                kept[k] = source[table[k, 1]]


def correction_kernel(
    entries, sums, near, far, across, image, wave, image_out, out, ratio, result, sems
):
    chunks = sems.shape[0] - 1
    size = image.shape[0] // chunks

    def total(ref):
        parts = [[ref[base + n : base + n + 1, 0:1] for n in range(4)] for base in (0, 8, 16, 24)]
        return merged(merged(*parts[:2]), merged(*parts[2:]))

    whole = merged(merged(total(sums), total(near)), merged(total(far), total(across)))
    rayleigh = whole[3] / whole[0]
    gap = ratio_of(whole[0], whole[1]) - rayleigh
    scale = lax.rsqrt((whole[2] + gap * gap * whole[0]) / entries + 1e-06)
    ratio[0] = rayleigh[0, 0]
    copies = [pltpu.make_async_copy(image, image_out, sems.at[chunks])]
    copies[0].start()
    for n in range(chunks):
        part = pl.ds(n * size, size)
        result[part] = (image[part] - rayleigh * wave[part].astype(jnp.float32)) * scale
        copies.append(pltpu.make_async_copy(result.at[part], out.at[part], sems.at[n]))
        copies[-1].start()
    for copy in copies:
        copy.wait()


def ratio_of(norm, correlation):
    return jnp.where(norm > 0, correlation / jnp.where(norm > 0, norm, 1.0), 0.0)


def merged(one, two):
    low, high = jnp.minimum(one[0], two[0]), jnp.maximum(one[0], two[0])
    norm = one[0] + two[0]
    gap = ratio_of(one[0], one[1]) - ratio_of(two[0], two[1])
    shared = low * jnp.where(norm > 0, high / jnp.where(norm > 0, norm, 1.0), 0.0)
    return norm, one[1] + two[1], one[2] + two[2] + gap * gap * shared, one[3] + two[3]


def ranks(key):
    at = jnp.arange(key.shape[-1])
    mine, others = key[..., :, None], key[..., None, :]
    before = (others < mine) | ((others == mine) & (at[None, :] < at[:, None]))
    return jnp.sum(before.astype(jnp.int32), axis=-1)


def call(kernel, out_shape, in_spaces, out_spaces, scratch, flops=1, aliases={}, vmem=VMEM_LIMIT):
    return pl.pallas_call(
        kernel,
        out_shape=out_shape,
        in_specs=[pl.BlockSpec(memory_space=space) for space in in_spaces],
        out_specs=jax.tree.map(lambda space: pl.BlockSpec(memory_space=space), out_spaces),
        scratch_shapes=scratch,
        input_output_aliases=aliases,
        compiler_params=pltpu.CompilerParams(vmem_limit_bytes=vmem),
        cost_estimate=pl.CostEstimate(
            flops=flops, bytes_accessed=1, transcendentals=0
        ),
    )


def after(array, *others):
    return lax.optimization_barrier((array, *others))[0]


def on_device(
    wavefunction,
    left_sector,
    right_sector,
    phys_index,
    left_environment,
    right_environment,
    term_weights,
):
    blocks, dim, _ = wavefunction.shape
    terms, per_device = left_environment.shape[:2]
    most = 2 * max(1, blocks // 8)
    first_slots = blocks - most
    index = lax.axis_index("sector")
    z, y, c = index // 2, index % 2, lax.axis_index("term")
    flags = jnp.stack([z < 2, y != c, y == c]).astype(jnp.int32)

    def hop(array, step, where=lambda z, y, c: True):
        return move(array, pairs_of(step, where))

    def mine_of(own, swapped):
        return jnp.where(y == c, own, swapped)

    def tiled(facts):
        rows, columns = facts.shape
        return jnp.pad(facts.astype(bf16), ((0, dim - rows), (0, dim - columns)))[None]

    HBM, VMEM, SMEM = pltpu.HBM, pltpu.VMEM, pltpu.SMEM
    bf16, f32 = jnp.bfloat16, jnp.float32
    square = (dim, dim)
    env = (terms, per_device) + square
    info = jnp.stack([left_sector, right_sector - index * per_device, phys_index])
    parity = jnp.stack([c, c, 1 - c])[:, None]
    side = jnp.where(jnp.arange(2) == 0, y, 1 - y)

    def sorted_out(infos, count):
        left_device = infos[:, 0] // per_device
        step = left_device // 2 - z
        stage = jnp.where(step == 0, 0, jnp.where(step == -1, 1, jnp.where(step == 1, 2, 3)))
        here = left_device % 2 == parity[:count]
        guest = here & (jnp.abs(step) == 3)
        stage = jnp.where(here & ~guest, stage, -1)
        place = ranks(jnp.where(stage < 0, 0, jnp.where(stage == 3, 2, 1)))
        return here, guest, stage, place

    def ordered(places, rows, fields):
        chosen = (jnp.arange(rows)[None, :, None] == places[:, None, :]).astype(f32)
        values = jnp.stack(fields, axis=-1).astype(f32)
        return jnp.einsum("rsk,rkf->rsf", chosen, values, precision=lax.Precision.HIGHEST).astype(
            jnp.int32
        )

    weights_sib = move(term_weights, CORE)
    left_n = move(left_environment, DIAGONAL)
    left_n, weights_sib = lax.optimization_barrier((left_n, weights_sib))
    weights = mine_of(term_weights, weights_sib).astype(f32).T
    weights = jnp.broadcast_to(weights[:, :, None], weights.shape + (dim,)).reshape(-1, terms * dim)
    left_mine = mine_of(left_environment, left_n)
    below = hop(left_mine, up)
    above = hop(left_mine, down)

    right_n = move(after(right_environment, left_mine), DIAGONAL)
    right_mine = call(
        select_kernel,
        jax.ShapeDtypeStruct(env, bf16),
        [SMEM, HBM, HBM],
        HBM,
        [pltpu.VMEM(env, bf16), pltpu.SemaphoreType.DMA((2, terms))],
    )(flags, right_environment, right_n)
    info_other = move(after(info, left_mine), COLUMN)

    block = jnp.arange(blocks)
    _, guest, _, _ = sorted_out(info[None], 1)
    guest_place = ranks(jnp.where(guest, 0, 1))
    guest_fields = [jnp.where(guest, 3, -1), block[None], info[None, 0] % per_device]
    guest_fields += [jnp.broadcast_to(side[:1, None] != c, (1, blocks)), info[None, 1], info[None, 2]]
    guest_table = ordered(guest_place, most, guest_fields)[0]
    picked = call(
        pick_kernel,
        jax.ShapeDtypeStruct((most + 1,) + square, bf16),
        [SMEM, VMEM, VMEM],
        VMEM,
        [],
    )(guest_table, after(wavefunction, info_other), tiled(guest_table))
    wave_guest = move(after(picked, left_mine), GUEST)

    infos = jnp.stack([info, info_other, info])
    here, guest, stage, place = sorted_out(infos, 3)
    guest_place = ranks(jnp.where(guest, 0, 1))
    table = ordered(
        place[:2],
        blocks,
        [
            stage[:2],
            jnp.broadcast_to(block, (2, blocks)),
            infos[:2, 0] % per_device,
            jnp.broadcast_to(side[:, None] != c, (2, blocks)),
            infos[:2, 1],
            infos[:2, 2],
        ],
    )
    far_table = table[:, first_slots:].reshape(2 * most, -1)
    table = table.reshape(2 * blocks, -1)
    table = table.reshape(2, blocks, -1)

    def source_of(which, of):
        late_place = jnp.where(guest[of], most + guest_place[of], place[of] - first_slots)
        late = guest[of] | (place[of] >= first_slots)
        return jnp.stack(
            [2 * which + late.astype(jnp.int32), jnp.where(late, late_place, place[of])], axis=-1
        )

    sources = jnp.where(here[0][:, None], source_of(0, 0), source_of(1, 2))
    picked_out = jnp.stack([sources[:, 0] == 0, sources[:, 0] == 1]).astype(jnp.int32)
    first_table, late_table = ordered(
        ranks(1 - picked_out),
        blocks,
        [
            picked_out,
            jnp.broadcast_to(block, (2, blocks)),
            jnp.broadcast_to(sources[:, 1], (2, blocks)),
        ],
    )

    held = (below, above, right_mine, wave_guest)
    held += (table, far_table, weights, sources, first_table, late_table, flags)
    held = lax.optimization_barrier(held)
    below, above, right_mine, wave_guest = held[:4]
    table, far_table, weights, sources, first_table, late_table, flags = held[4:]
    right_guest = hop(right_mine, inward, outer)
    below_two = hop(below, up, inner)
    above_two = hop(above, down, inner)
    wave_other = move(after(wavefunction, right_mine), COLUMN)
    right_sib = move(right_mine, CORE)
    map_shape = jax.ShapeDtypeStruct((8, 128), f32)

    def near(relation, blocks_of, kind):
        return call(
            near_kernel,
            (
                jax.ShapeDtypeStruct((first_slots,) + square, kind),
                jax.ShapeDtypeStruct((most,) + square, kind),
                jax.ShapeDtypeStruct((most, dim, terms * dim), bf16),
                map_shape,
            ),
            [SMEM] + [HBM] * 7,
            (HBM, HBM, HBM, VMEM),
            [
                pltpu.VMEM(weights.shape, f32),
                pltpu.VMEM((blocks,) + square, kind),
                pltpu.VMEM((most, dim, terms * dim), bf16),
                pltpu.VMEM((blocks,) + square, bf16),
                pltpu.VMEM((2,) + env, bf16),
                pltpu.VMEM((3,) + env, bf16),
                pltpu.SemaphoreType.DMA((9,)),
                pltpu.SemaphoreType.DMA((most,)),
            ],
        )(
            table[relation], weights, blocks_of, right_mine, right_sib,
            left_mine, below, above,
        )

    own, own_last, carried_own, map_own = near(0, wavefunction, f32)
    other, other_last, carried_other, map_other = near(1, wave_other, bf16)
    wave_guest_other = move(after(wave_guest, own), COLUMN_INNER)
    guest_got = jnp.concatenate(
        [guests[most, :most, :6] for guests in (wave_guest, wave_guest_other)]
    ).astype(jnp.int32)
    held = (right_guest, below_two, above_two, wave_guest_other)
    held += (own, own_last, carried_own, other, other_last, carried_other, guest_got)
    held = lax.optimization_barrier(held)
    right_guest, below_two, above_two, wave_guest_other = held[:4]
    own, own_last, carried_own, other, other_last, carried_other, guest_got = held[4:]
    first_got = move(other, COLUMN)
    right_guest_sib = hop(right_guest, other_core, inner)
    last = jax.ShapeDtypeStruct((most,) + square, f32)
    last_sent = jax.ShapeDtypeStruct((most,) + square, bf16)
    guest_own, guest_other, map_guest = call(
        guest_kernel,
        (last_sent, last_sent, map_shape),
        [SMEM] * 2 + [HBM] * 7,
        (VMEM,) * 3,
        [
            pltpu.VMEM(weights.shape, f32),
            pltpu.VMEM((2 * most,) + square, bf16),
            pltpu.VMEM((2,) + env, bf16),
            pltpu.VMEM(env, bf16),
            pltpu.SemaphoreType.DMA((6,)),
        ],
        vmem=VMEM_SMALL,
    )(
        flags, guest_got, weights, below_two, above_two,
        wave_guest, wave_guest_other, right_guest, right_guest_sib,
    )
    guest_straight = move(guest_own, GUEST_BACK)
    guest_crossed = move(guest_other, GUEST_BACK_CROSSED)
    last_own, last_other, map_far = call(
        far_kernel,
        (last, last_sent, map_shape),
        [SMEM] * 2 + [HBM] * 8,
        (VMEM,) * 3,
        [
            pltpu.VMEM((2 * most, dim, terms * dim), bf16),
            pltpu.VMEM((2 * most,) + square, bf16),
            pltpu.VMEM(env, bf16),
            pltpu.SemaphoreType.DMA((2 * most,)),
            pltpu.SemaphoreType.DMA((2 * most,)),
            pltpu.SemaphoreType.DMA((3,)),
        ],
        2**37,
    )(
        flags, after(far_table, guest_own), carried_own, carried_other, below_two, above_two,
        own_last, other_last, wavefunction, wave_other,
    )
    last_got = move(last_other, COLUMN)
    first_own, sums_first = call(
        first_kernel,
        (jax.ShapeDtypeStruct((first_slots,) + square, f32), jax.ShapeDtypeStruct((8, 128), f32)),
        [SMEM] + [VMEM] * 3,
        (VMEM, VMEM),
        [],
        vmem=VMEM_SMALL,
    )(first_table, own, after(first_got, last_own), wavefunction)
    first_sib = move(first_own, CORE)
    guest_full = call(sum_kernel, last, [VMEM] * 2, VMEM, [], 2**30, vmem=VMEM_SMALL)(
        after(guest_straight, sums_first), guest_crossed
    )
    late, sums = call(
        late_kernel,
        (jax.ShapeDtypeStruct((2 * most,) + square, f32), jax.ShapeDtypeStruct((8, 128), f32)),
        [SMEM] + [VMEM] * 9,
        (VMEM, VMEM),
        [],
        vmem=VMEM_SMALL,
    )(
        late_table, sums_first, last_own, last_got, guest_full, wavefunction,
        map_own, map_other, map_guest, map_far,
    )
    sums = jnp.concatenate([sums] + [move(sums, pairs) for pairs in (CORE, COLUMN, ACROSS)])
    late_sib = move(after(late, sums), CORE)
    image_shape = jax.ShapeDtypeStruct((blocks,) + square, f32)
    kept = call(
        place_kernel,
        image_shape,
        [SMEM] + [VMEM] * 4,
        VMEM,
        [],
        vmem=VMEM_SMALL,
    )(sources, first_own, late, first_sib, late_sib)
    sums = [sums] + [move(sums, pairs_of(lambda z, y, c: (z ^ n, y, c))) for n in (1, 2, 3)]
    image, correction, rayleigh = call(
        functools.partial(correction_kernel, blocks * 8 * dim * dim),
        (image_shape, image_shape, jax.ShapeDtypeStruct((1,), f32)),
        [VMEM] * 6,
        (HBM, HBM, SMEM),
        [pltpu.VMEM((blocks,) + square, f32), pltpu.SemaphoreType.DMA((9,))],
        vmem=VMEM_SMALL,
    )(*sums, kept, wavefunction)
    return image, correction, rayleigh


def solution(mesh):
    placed = (
        P(("parts", "sector"), None, None),
        P(("parts", "sector")),
        P(("parts", "sector")),
        P(("parts", "sector")),
        P(("parts", "term"), "sector", None, None),
        P(("parts", "term"), "sector", None, None),
        P(("parts", "term"), None),
    )
    paired = mesh.shape["sector"] == 8 and mesh.shape["term"] == 2
    return jax.shard_map(
        on_device if paired else on_device_any,
        mesh=mesh,
        in_specs=placed,
        out_specs=(
            P(("parts", "sector"), None, None),
            P(("parts", "sector"), None, None),
            P("parts"),
        ),
        check_vma=False,
    )
```

```python
import functools

import jax
import jax.numpy as jnp
from jax import lax
from jax.experimental import pallas as pl
from jax.experimental.pallas import tpu as pltpu
from jax.sharding import PartitionSpec as P

BOTH = ("sector", "term")
VMEM_LIMIT = 60 * 2**20
VMEM_SMALL = 32 * 2**20


def on_device_any(
    wavefunction,
    left_sector,
    right_sector,
    phys_index,
    left_environment,
    right_environment,
    term_weights,
):
    blocks = wavefunction.shape[0]
    sector_dim = wavefunction.shape[1]
    sector_count = lax.axis_size("sector")
    per_device = right_environment.shape[1]
    capacity = 2 * max(1, blocks // sector_count)
    own_index = lax.axis_index("sector")
    right_local = right_sector - own_index * per_device
    target = left_sector // per_device
    positions = jnp.arange(blocks)
    earlier = (target[None, :] == target[:, None]) & (positions[None, :] < positions[:, None])
    placement_order = jnp.sum(earlier.astype(jnp.int32), axis=1)
    physical_selector_matrix = (
        phys_index[:, None] == jnp.arange(term_weights.shape[1])[None, :]
    ).astype(jnp.bfloat16)
    slot_index = target * capacity + placement_order
    slot_count = sector_count * capacity
    selector_f = (jnp.arange(slot_count)[:, None] == slot_index[None, :]).astype(jnp.float32)
    wanted = jnp.dot(
        selector_f, (left_sector % per_device).astype(jnp.float32), precision=lax.Precision.HIGHEST
    ).astype(jnp.int32)
    requests = lax.all_to_all(
        wanted.reshape(sector_count, capacity), "sector", split_axis=0, concat_axis=0, tiled=True
    )
    picked = jnp.take(left_environment, requests.reshape(-1), axis=1)
    picked = jnp.moveaxis(picked, 0, 1).reshape(
        sector_count, capacity, left_environment.shape[0], sector_dim, sector_dim
    )
    fetched = lax.all_to_all(picked, "sector", split_axis=0, concat_axis=0, tiled=True)
    left_blocks = jnp.take(
        fetched.reshape(slot_count, left_environment.shape[0], sector_dim, sector_dim),
        slot_index,
        axis=0,
    )
    right_taken = jnp.take(right_environment, right_local, axis=1)
    block_weights = jnp.dot(
        physical_selector_matrix, term_weights.T, preferred_element_type=jnp.float32
    )
    environment_product = jnp.einsum(
        "kab,tkcb->ktac", wavefunction, right_taken, preferred_element_type=jnp.float32
    )
    carried = (environment_product * block_weights[:, :, None, None]).astype(jnp.bfloat16)
    image_partial_result = jnp.einsum(
        "ktij,ktjc->kic", left_blocks, carried, preferred_element_type=jnp.float32
    )
    image = lax.psum(image_partial_result, "term")
    wave_f32 = wavefunction.astype(jnp.float32)
    norm_wave = jnp.sum(wave_f32 * wave_f32)
    correlation = jnp.sum(wave_f32 * image)
    entries = blocks * sector_count * sector_dim * sector_dim
    norm_all, correlation_all = lax.psum((norm_wave, correlation), "sector")
    rayleigh = correlation_all / norm_all
    residual = image - rayleigh * wave_f32
    norm_resid = lax.psum(jnp.sum(residual * residual), "sector")
    correction = residual * lax.rsqrt(norm_resid / entries + 1e-06)
    return (image, correction, jnp.reshape(rayleigh, (1,)))


def pairs_of(target, chosen=lambda z, y, c: True):
    found = []
    for z in range(4):
        for y in range(2):
            for c in range(2):
                if chosen(z, y, c):
                    to = target(z, y, c)
                    if 0 <= to[0] < 4:
                        found.append(((z * 2 + y) * 2 + c, (to[0] * 2 + to[1]) * 2 + to[2]))
    return found


def inner(z, y, c):
    return z in (1, 2)


def outer(z, y, c):
    return z in (0, 3)


def straight(z, y, c):
    return y == c


def crossed(z, y, c):
    return y != c


def both(one, two):
    return lambda z, y, c: one(z, y, c) and two(z, y, c)


def up(z, y, c):
    return z + 1, y, c


def down(z, y, c):
    return z - 1, y, c


def other_core(z, y, c):
    return z, y, 1 - c


def other_column(z, y, c):
    return z, 1 - y, c


def inward(z, y, c):
    return (1 if z == 0 else 2), y, c


def outward(z, y, c):
    return (0 if z == 1 else 3), y, c


def outward_crossed(z, y, c):
    return (0 if z == 1 else 3), 1 - y, c


DIAGONAL = pairs_of(lambda z, y, c: (z, 1 - y, 1 - c), crossed)
CORE = pairs_of(other_core)
COLUMN = pairs_of(other_column)
ACROSS = pairs_of(lambda z, y, c: (z, 1 - y, 1 - c))
COLUMN_INNER = pairs_of(other_column, inner)
GUEST = pairs_of(inward, outer)
GUEST_BACK = pairs_of(outward, inner)
GUEST_BACK_CROSSED = pairs_of(outward_crossed, inner)


def move(array, pairs):
    return lax.ppermute(array, BOTH, pairs)


def carried_of(wave, right, weights):
    terms, dim, _ = right.shape
    product = lax.dot_general(
        wave,
        right.reshape(terms * dim, dim),
        (((1,), (1,)), ((), ())),
        preferred_element_type=jnp.float32,
    )
    return (product * weights).astype(jnp.bfloat16)


def applied(left, carried):
    terms, dim, _ = left.shape
    lefts = jnp.concatenate([left[t] for t in range(terms)], axis=1)
    stacked = jnp.concatenate(
        [carried[:, t * dim : (t + 1) * dim] for t in range(terms)], axis=0
    )
    return jnp.dot(lefts, stacked, preferred_element_type=jnp.float32)


def choose(flag, one, two, target, sem):
    @pl.when(flag)
    def _():
        pltpu.make_async_copy(one, target, sem).start()

    @pl.when(jnp.logical_not(flag))
    def _():
        pltpu.make_async_copy(two, target, sem).start()


def grouped(low, high, step, body):
    @pl.loop(0, (high - low + step - 1) // step)
    def _(group):
        for n in range(step):
            row = low + group * step + n
            body(jnp.minimum(row, high - 1), (row < high).astype(jnp.float32))


def folded(value):
    return jnp.sum(value.reshape(-1, 8, 128), axis=0)


def paired(found, wave, counted):
    return folded(found * wave.astype(jnp.float32)) * counted


def count_of(table, base, rows, stage):
    def add(row, total):
        return total + (table[base + row, 0] == stage).astype(jnp.int32)

    return lax.fori_loop(0, rows, add, jnp.int32(0))


def select_kernel(flags, straight_side, crossed_side, out, held, sems):
    terms = held.shape[0]
    outs = [pltpu.make_async_copy(held.at[t], out.at[t], sems.at[1, t]) for t in range(terms)]
    for t in range(terms):
        choose(flags[2] == 1, straight_side.at[t], crossed_side.at[t], held.at[t], sems.at[0, t])
    for t in range(terms):
        pltpu.make_async_copy(straight_side.at[t], held.at[t], sems.at[0, t]).wait()
        outs[t].start()
    for t in range(terms):
        outs[t].wait()


def near_kernel(
    table, weights_in, wave_in, right_mine, right_sib, left_mine, below, above,
    first, last, carried_out, correlation,
    weights, result, carried, wave, right, left, sems, carried_sems,
):
    blocks = wave.shape[0]
    most = last.shape[0]
    first_slots = blocks - most
    copies = [
        pltpu.make_async_copy(source, target, sems.at[n])
        for n, (source, target) in enumerate(
            (
                (wave_in, wave),
                (right_mine, right.at[0]),
                (right_sib, right.at[1]),
                (weights_in, weights),
                (left_mine, left.at[0]),
                (below, left.at[1]),
                (above, left.at[2]),
            )
        )
    ]
    for copy in copies:
        copy.start()
    result[...] = jnp.zeros_like(result)
    correlation[...] = jnp.zeros_like(correlation)
    skipped = count_of(table, 0, blocks, -1)
    end = blocks - count_of(table, 0, blocks, 3)
    for copy in copies[:4]:
        copy.wait()

    def carry(slot):
        return carried_of(
            wave[table[slot, 1]], right[table[slot, 3], :, table[slot, 4]], weights[pl.ds(table[slot, 5], 1), :]
        )

    def written(slot):
        at = slot - first_slots
        return pltpu.make_async_copy(carried.at[at], carried_out.at[at], carried_sems.at[at])

    def keep(slot, _):
        carried[slot - first_slots] = carry(slot)

    grouped(end, blocks, 4, keep)

    @pl.loop(end, blocks)
    def _(slot):
        written(slot).start()

    for copy in copies[4:]:
        copy.wait()

    def apply(slot, counted):
        found = applied(left[table[slot, 0], :, table[slot, 2]], carry(slot))
        result[slot] = found.astype(result.dtype)
        correlation[...] += paired(found, wave[table[slot, 1]], counted)

    grouped(skipped, end, 4, apply)
    outs = [
        pltpu.make_async_copy(result.at[part], target, sems.at[len(copies) + n])
        for n, (part, target) in enumerate(
            ((pl.ds(0, first_slots), first), (pl.ds(first_slots, most), last))
        )
    ]
    for out in outs:
        out.start()
    for out in outs:
        out.wait()

    @pl.loop(end, blocks)
    def _(slot):
        written(slot).wait()


def guest_kernel(
    flags, table, weights_in, below, above, wave_own, wave_other, right_mine, right_sib,
    own_out, other_out, correlation,
    weights, wave, right, left, sems,
):
    half = own_out.shape[0]
    counts = [count_of(table, part * half, half, 3) for part in range(2)]
    copies = [
        pltpu.make_async_copy(source, target, sems.at[n])
        for n, (source, target) in enumerate(
            (
                (right_mine, right.at[0]),
                (right_sib, right.at[1]),
                (wave_own.at[pl.ds(0, half)], wave.at[pl.ds(0, half)]),
                (wave_other.at[pl.ds(0, half)], wave.at[pl.ds(half, half)]),
                (weights_in, weights),
            )
        )
    ]

    @pl.when(counts[0] + counts[1] > 0)
    def _():
        for copy in copies:
            copy.start()
        choose(flags[0] == 1, above, below, left, sems.at[len(copies)])

    own_out[...] = jnp.zeros_like(own_out)
    other_out[...] = jnp.zeros_like(other_out)
    correlation[...] = jnp.zeros_like(correlation)

    @pl.when(counts[0] + counts[1] > 0)
    def _():
        for copy in copies:
            copy.wait()
        pltpu.make_async_copy(above, left, sems.at[len(copies)]).wait()

    for part, target in enumerate((own_out, other_out)):

        def apply(row, counted):
            carried = carried_of(
                wave[row],
                right[flags[1 + part], :, table[row, 4]],
                weights[pl.ds(table[row, 5], 1), :],
            )
            result = applied(left[:, table[row, 2]], carried)
            target[row - part * half] = result.astype(target.dtype)
            correlation[...] += paired(result, wave[row], counted)

        grouped(part * half, part * half + counts[part], 4, apply)


def far_kernel(
    flags, table, carried_own, carried_other, below, above, own, other, wave_own, wave_other,
    own_out, other_out, correlation,
    held, wave, left, sems, wave_sems, more_sems,
):
    half = own_out.shape[0]
    lows = [half - count_of(table, part * half, half, 3) for part in range(2)]
    choose(flags[0] == 1, above, below, left, more_sems.at[0])
    kept = [
        pltpu.make_async_copy(source, target, more_sems.at[1 + n])
        for n, (source, target) in enumerate(((own, own_out), (other, other_out)))
    ]
    for copy in kept:
        copy.start()
    for part, (carried, waves) in enumerate(((carried_own, wave_own), (carried_other, wave_other))):

        @pl.loop(lows[part], half)
        def _(slot):
            row = part * half + slot
            pltpu.make_async_copy(carried.at[slot], held.at[row], sems.at[row]).start()
            pltpu.make_async_copy(waves.at[table[row, 1]], wave.at[row], wave_sems.at[row]).start()

    correlation[...] = jnp.zeros_like(correlation)
    for copy in kept:
        copy.wait()
    pltpu.make_async_copy(above, left, more_sems.at[0]).wait()
    for part, (carried, target) in enumerate(((carried_other, other_out), (carried_own, own_out))):
        part = 1 - part

        @pl.loop(lows[part], half)
        def _(slot):
            row = part * half + slot
            pltpu.make_async_copy(carried.at[slot], held.at[row], sems.at[row]).wait()
            pltpu.make_async_copy(wave_own.at[0], wave.at[row], wave_sems.at[row]).wait()

        def apply(slot, counted):
            row = part * half + slot
            result = applied(left[:, table[row, 2]], held[row])
            target[slot] = result.astype(target.dtype)
            correlation[...] += paired(result, wave[row], counted)

        grouped(lows[part], half, 4, apply)


def pick_kernel(table, own, facts, out):
    slots = out.shape[0] - 1
    out[slots] = facts[0]

    @pl.loop(0, slots)
    def _(slot):
        out[slot] = own[table[slot, 1]]


def first_kernel(table, own, got, wave, whole, sums):
    blocks = wave.shape[0]
    zero = jnp.zeros((8, 128), jnp.float32)
    whole[...] = own[...] + got[...].astype(jnp.float32)
    count = count_of(table, 0, blocks, 1)

    def add(n, totals):
        value, found = wave[table[n, 1]].astype(jnp.float32), whole[table[n, 2]]
        return totals[0] + folded(value * value), totals[1] + folded(value * found)

    norm_map, correlation_map = lax.fori_loop(0, count, add, (zero, zero))
    norm = jnp.sum(norm_map, keepdims=True)
    correlation = jnp.sum(correlation_map, keepdims=True)
    ratio = ratio_of(norm, correlation)

    def rest(n, total):
        residual = whole[table[n, 2]] - ratio * wave[table[n, 1]].astype(jnp.float32)
        return total + folded(residual * residual)

    resid = jnp.sum(lax.fori_loop(0, count, rest, zero), keepdims=True)
    sums[...] = lined(norm, correlation, resid)


def lined(*values):
    line = lax.broadcasted_iota(jnp.int32, (8, 128), 0)
    result = jnp.zeros((8, 128), jnp.float32)
    for n, value in enumerate(values):
        result = jnp.where(line == n, value, result)
    return result


def sum_kernel(one, two, out):
    out[...] = one[...].astype(out.dtype) + two[...].astype(out.dtype)


def late_kernel(
    table, sums_first, last_own, last_got, guest_full, wave, map_a, map_b, map_c, map_d, late, sums
):
    blocks = wave.shape[0]
    most = last_own.shape[0]
    zero = jnp.zeros((8, 128), jnp.float32)
    late[pl.ds(0, most)] = last_own[...] + last_got[...].astype(jnp.float32)
    late[pl.ds(most, most)] = guest_full[...]
    count = count_of(table, 0, blocks, 1)

    def add(n, totals):
        value, found = wave[table[n, 1]].astype(jnp.float32), late[table[n, 2]]
        return totals[0] + folded(value * value), totals[1] + folded(value * found)

    norm_map, correlation_map = lax.fori_loop(0, count, add, (zero, zero))
    norm = jnp.sum(norm_map, keepdims=True)
    correlation = jnp.sum(correlation_map, keepdims=True)
    ratio = ratio_of(norm, correlation)

    def rest(n, total):
        residual = late[table[n, 2]] - ratio * wave[table[n, 1]].astype(jnp.float32)
        return total + folded(residual * residual)

    resid = jnp.sum(lax.fori_loop(0, count, rest, zero), keepdims=True)
    first = [sums_first[n : n + 1, 0:1] for n in range(4)]
    exact = jnp.sum(map_a[...] + map_b[...] + map_c[...] + map_d[...], keepdims=True)
    sums[...] = lined(*merged(first, (norm, correlation, resid, exact)))


def place_kernel(table, first_own, late_own, first_sib, late_sib, kept):
    @pl.loop(0, kept.shape[0])
    def _(k):
        for code, source in enumerate((first_own, late_own, first_sib, late_sib)):

            @pl.when(table[k, 0] == code)
            def _():
                kept[k] = source[table[k, 1]]


def correction_kernel(
    entries, sums, near, far, across, image, wave, image_out, out, ratio, result, sems
):
    chunks = sems.shape[0] - 1
    size = image.shape[0] // chunks

    def total(ref):
        parts = [[ref[base + n : base + n + 1, 0:1] for n in range(4)] for base in (0, 8, 16, 24)]
        return merged(merged(*parts[:2]), merged(*parts[2:]))

    whole = merged(merged(total(sums), total(near)), merged(total(far), total(across)))
    rayleigh = whole[3] / whole[0]
    gap = ratio_of(whole[0], whole[1]) - rayleigh
    scale = lax.rsqrt((whole[2] + gap * gap * whole[0]) / entries + 1e-06)
    ratio[0] = rayleigh[0, 0]
    copies = [pltpu.make_async_copy(image, image_out, sems.at[chunks])]
    copies[0].start()
    for n in range(chunks):
        part = pl.ds(n * size, size)
        result[part] = (image[part] - rayleigh * wave[part].astype(jnp.float32)) * scale
        copies.append(pltpu.make_async_copy(result.at[part], out.at[part], sems.at[n]))
        copies[-1].start()
    for copy in copies:
        copy.wait()


def ratio_of(norm, correlation):
    return jnp.where(norm > 0, correlation / jnp.where(norm > 0, norm, 1.0), 0.0)


def merged(one, two):
    low, high = jnp.minimum(one[0], two[0]), jnp.maximum(one[0], two[0])
    norm = one[0] + two[0]
    gap = ratio_of(one[0], one[1]) - ratio_of(two[0], two[1])
    shared = low * jnp.where(norm > 0, high / jnp.where(norm > 0, norm, 1.0), 0.0)
    return norm, one[1] + two[1], one[2] + two[2] + gap * gap * shared, one[3] + two[3]


def ranks(key):
    at = jnp.arange(key.shape[-1])
    mine, others = key[..., :, None], key[..., None, :]
    before = (others < mine) | ((others == mine) & (at[None, :] < at[:, None]))
    return jnp.sum(before.astype(jnp.int32), axis=-1)


def call(kernel, out_shape, in_spaces, out_spaces, scratch, flops=1, aliases={}, vmem=VMEM_LIMIT):
    return pl.pallas_call(
        kernel,
        out_shape=out_shape,
        in_specs=[pl.BlockSpec(memory_space=space) for space in in_spaces],
        out_specs=jax.tree.map(lambda space: pl.BlockSpec(memory_space=space), out_spaces),
        scratch_shapes=scratch,
        input_output_aliases=aliases,
        compiler_params=pltpu.CompilerParams(vmem_limit_bytes=vmem),
        cost_estimate=pl.CostEstimate(
            flops=flops, bytes_accessed=1, transcendentals=0
        ),
    )


def after(array, *others):
    return lax.optimization_barrier((array, *others))[0]


def on_device(
    wavefunction,
    left_sector,
    right_sector,
    phys_index,
    left_environment,
    right_environment,
    term_weights,
):
    blocks, dim, _ = wavefunction.shape
    terms, per_device = left_environment.shape[:2]
    most = 2 * max(1, blocks // 8)
    first_slots = blocks - most
    index = lax.axis_index("sector")
    z, y, c = index // 2, index % 2, lax.axis_index("term")
    flags = jnp.stack([z < 2, y != c, y == c]).astype(jnp.int32)

    def hop(array, step, where=lambda z, y, c: True):
        return move(array, pairs_of(step, where))

    def mine_of(own, swapped):
        return jnp.where(y == c, own, swapped)

    def tiled(facts):
        rows, columns = facts.shape
        return jnp.pad(facts.astype(bf16), ((0, dim - rows), (0, dim - columns)))[None]

    HBM, VMEM, SMEM = pltpu.HBM, pltpu.VMEM, pltpu.SMEM
    bf16, f32 = jnp.bfloat16, jnp.float32
    square = (dim, dim)
    env = (terms, per_device) + square
    info = jnp.stack([left_sector, right_sector - index * per_device, phys_index])
    parity = jnp.stack([c, c, 1 - c])[:, None]
    side = jnp.where(jnp.arange(2) == 0, y, 1 - y)

    def sorted_out(infos, count):
        left_device = infos[:, 0] // per_device
        step = left_device // 2 - z
        stage = jnp.where(step == 0, 0, jnp.where(step == -1, 1, jnp.where(step == 1, 2, 3)))
        here = left_device % 2 == parity[:count]
        guest = here & (jnp.abs(step) == 3)
        stage = jnp.where(here & ~guest, stage, -1)
        place = ranks(jnp.where(stage < 0, 0, jnp.where(stage == 3, 2, 1)))
        return here, guest, stage, place

    def ordered(places, rows, fields):
        chosen = (jnp.arange(rows)[None, :, None] == places[:, None, :]).astype(f32)
        values = jnp.stack(fields, axis=-1).astype(f32)
        return jnp.einsum("rsk,rkf->rsf", chosen, values, precision=lax.Precision.HIGHEST).astype(
            jnp.int32
        )

    weights_sib = move(term_weights, CORE)
    left_n = move(left_environment, DIAGONAL)
    left_n, weights_sib = lax.optimization_barrier((left_n, weights_sib))
    weights = mine_of(term_weights, weights_sib).astype(f32).T
    weights = jnp.broadcast_to(weights[:, :, None], weights.shape + (dim,)).reshape(-1, terms * dim)
    left_mine = mine_of(left_environment, left_n)
    below = hop(left_mine, up)
    above = hop(left_mine, down)

    right_n = move(after(right_environment, left_n), DIAGONAL)
    right_mine = call(
        select_kernel,
        jax.ShapeDtypeStruct(env, bf16),
        [SMEM, HBM, HBM],
        HBM,
        [pltpu.VMEM(env, bf16), pltpu.SemaphoreType.DMA((2, terms))],
    )(flags, right_environment, right_n)
    info_other = move(after(info, left_mine), COLUMN)

    block = jnp.arange(blocks)
    _, guest, _, _ = sorted_out(info[None], 1)
    guest_place = ranks(jnp.where(guest, 0, 1))
    guest_fields = [jnp.where(guest, 3, -1), block[None], info[None, 0] % per_device]
    guest_fields += [jnp.broadcast_to(side[:1, None] != c, (1, blocks)), info[None, 1], info[None, 2]]
    guest_table = ordered(guest_place, most, guest_fields)[0]
    picked = call(
        pick_kernel,
        jax.ShapeDtypeStruct((most + 1,) + square, bf16),
        [SMEM, VMEM, VMEM],
        VMEM,
        [],
    )(guest_table, after(wavefunction, info_other), tiled(guest_table))
    wave_guest = move(after(picked, left_mine), GUEST)

    infos = jnp.stack([info, info_other, info])
    here, guest, stage, place = sorted_out(infos, 3)
    guest_place = ranks(jnp.where(guest, 0, 1))
    table = ordered(
        place[:2],
        blocks,
        [
            stage[:2],
            jnp.broadcast_to(block, (2, blocks)),
            infos[:2, 0] % per_device,
            jnp.broadcast_to(side[:, None] != c, (2, blocks)),
            infos[:2, 1],
            infos[:2, 2],
        ],
    )
    far_table = table[:, first_slots:].reshape(2 * most, -1)
    table = table.reshape(2 * blocks, -1)
    table = table.reshape(2, blocks, -1)

    def source_of(which, of):
        late_place = jnp.where(guest[of], most + guest_place[of], place[of] - first_slots)
        late = guest[of] | (place[of] >= first_slots)
        return jnp.stack(
            [2 * which + late.astype(jnp.int32), jnp.where(late, late_place, place[of])], axis=-1
        )

    sources = jnp.where(here[0][:, None], source_of(0, 0), source_of(1, 2))
    picked_out = jnp.stack([sources[:, 0] == 0, sources[:, 0] == 1]).astype(jnp.int32)
    first_table, late_table = ordered(
        ranks(1 - picked_out),
        blocks,
        [
            picked_out,
            jnp.broadcast_to(block, (2, blocks)),
            jnp.broadcast_to(sources[:, 1], (2, blocks)),
        ],
    )

    held = (below, above, right_mine, wave_guest)
    held += (table, far_table, weights, sources, first_table, late_table, flags)
    held = lax.optimization_barrier(held)
    below, above, right_mine, wave_guest = held[:4]
    table, far_table, weights, sources, first_table, late_table, flags = held[4:]
    right_guest = hop(right_mine, inward, outer)
    below_two = hop(below, up, inner)
    above_two = hop(above, down, inner)
    wave_other = move(after(wavefunction, right_mine), COLUMN)
    right_sib = move(right_mine, CORE)
    map_shape = jax.ShapeDtypeStruct((8, 128), f32)

    def near(relation, blocks_of, kind):
        return call(
            near_kernel,
            (
                jax.ShapeDtypeStruct((first_slots,) + square, kind),
                jax.ShapeDtypeStruct((most,) + square, kind),
                jax.ShapeDtypeStruct((most, dim, terms * dim), bf16),
                map_shape,
            ),
            [SMEM] + [HBM] * 7,
            (HBM, HBM, HBM, VMEM),
            [
                pltpu.VMEM(weights.shape, f32),
                pltpu.VMEM((blocks,) + square, kind),
                pltpu.VMEM((most, dim, terms * dim), bf16),
                pltpu.VMEM((blocks,) + square, bf16),
                pltpu.VMEM((2,) + env, bf16),
                pltpu.VMEM((3,) + env, bf16),
                pltpu.SemaphoreType.DMA((9,)),
                pltpu.SemaphoreType.DMA((most,)),
            ],
        )(
            table[relation], weights, blocks_of, right_mine, right_sib,
            left_mine, below, above,
        )

    own, own_last, carried_own, map_own = near(0, wavefunction, f32)
    other, other_last, carried_other, map_other = near(1, wave_other, bf16)
    wave_guest_other = move(after(wave_guest, own), COLUMN_INNER)
    guest_got = jnp.concatenate(
        [guests[most, :most, :6] for guests in (wave_guest, wave_guest_other)]
    ).astype(jnp.int32)
    held = (right_guest, below_two, above_two, wave_guest_other)
    held += (own, own_last, carried_own, other, other_last, carried_other, guest_got)
    held = lax.optimization_barrier(held)
    right_guest, below_two, above_two, wave_guest_other = held[:4]
    own, own_last, carried_own, other, other_last, carried_other, guest_got = held[4:]
    first_got = move(other, COLUMN)
    right_guest_sib = hop(right_guest, other_core, inner)
    last = jax.ShapeDtypeStruct((most,) + square, f32)
    last_sent = jax.ShapeDtypeStruct((most,) + square, bf16)
    guest_own, guest_other, map_guest = call(
        guest_kernel,
        (last_sent, last_sent, map_shape),
        [SMEM] * 2 + [HBM] * 7,
        (VMEM,) * 3,
        [
            pltpu.VMEM(weights.shape, f32),
            pltpu.VMEM((2 * most,) + square, bf16),
            pltpu.VMEM((2,) + env, bf16),
            pltpu.VMEM(env, bf16),
            pltpu.SemaphoreType.DMA((6,)),
        ],
        vmem=VMEM_SMALL,
    )(
        flags, guest_got, weights, below_two, above_two,
        wave_guest, wave_guest_other, right_guest, right_guest_sib,
    )
    guest_straight = move(guest_own, GUEST_BACK)
    guest_crossed = move(guest_other, GUEST_BACK_CROSSED)
    last_own, last_other, map_far = call(
        far_kernel,
        (last, last_sent, map_shape),
        [SMEM] * 2 + [HBM] * 8,
        (VMEM,) * 3,
        [
            pltpu.VMEM((2 * most, dim, terms * dim), bf16),
            pltpu.VMEM((2 * most,) + square, bf16),
            pltpu.VMEM(env, bf16),
            pltpu.SemaphoreType.DMA((2 * most,)),
            pltpu.SemaphoreType.DMA((2 * most,)),
            pltpu.SemaphoreType.DMA((3,)),
        ],
        2**37,
    )(
        flags, after(far_table, guest_own), carried_own, carried_other, below_two, above_two,
        own_last, other_last, wavefunction, wave_other,
    )
    last_got = move(last_other, COLUMN)
    first_own, sums_first = call(
        first_kernel,
        (jax.ShapeDtypeStruct((first_slots,) + square, f32), jax.ShapeDtypeStruct((8, 128), f32)),
        [SMEM] + [VMEM] * 3,
        (VMEM, VMEM),
        [],
        vmem=VMEM_SMALL,
    )(first_table, own, after(first_got, last_own), wavefunction)
    first_sib = move(first_own, CORE)
    guest_full = call(sum_kernel, last, [VMEM] * 2, VMEM, [], 2**30, vmem=VMEM_SMALL)(
        after(guest_straight, sums_first), guest_crossed
    )
    late, sums = call(
        late_kernel,
        (jax.ShapeDtypeStruct((2 * most,) + square, f32), jax.ShapeDtypeStruct((8, 128), f32)),
        [SMEM] + [VMEM] * 9,
        (VMEM, VMEM),
        [],
        vmem=VMEM_SMALL,
    )(
        late_table, sums_first, last_own, last_got, guest_full, wavefunction,
        map_own, map_other, map_guest, map_far,
    )
    sums = jnp.concatenate([sums] + [move(sums, pairs) for pairs in (CORE, COLUMN, ACROSS)])
    late_sib = move(after(late, sums), CORE)
    image_shape = jax.ShapeDtypeStruct((blocks,) + square, f32)
    kept = call(
        place_kernel,
        image_shape,
        [SMEM] + [VMEM] * 4,
        VMEM,
        [],
        vmem=VMEM_SMALL,
    )(sources, first_own, late, first_sib, late_sib)
    sums = [sums] + [move(sums, pairs_of(lambda z, y, c: (z ^ n, y, c))) for n in (1, 2, 3)]
    image, correction, rayleigh = call(
        functools.partial(correction_kernel, blocks * 8 * dim * dim),
        (image_shape, image_shape, jax.ShapeDtypeStruct((1,), f32)),
        [VMEM] * 6,
        (HBM, HBM, SMEM),
        [pltpu.VMEM((blocks,) + square, f32), pltpu.SemaphoreType.DMA((9,))],
        vmem=VMEM_SMALL,
    )(*sums, kept, wavefunction)
    return image, correction, rayleigh


def solution(mesh):
    placed = (
        P(("parts", "sector"), None, None),
        P(("parts", "sector")),
        P(("parts", "sector")),
        P(("parts", "sector")),
        P(("parts", "term"), "sector", None, None),
        P(("parts", "term"), "sector", None, None),
        P(("parts", "term"), None),
    )
    paired = mesh.shape["sector"] == 8 and mesh.shape["term"] == 2
    return jax.shard_map(
        on_device if paired else on_device_any,
        mesh=mesh,
        in_specs=placed,
        out_specs=(
            P(("parts", "sector"), None, None),
            P(("parts", "sector"), None, None),
            P("parts"),
        ),
        check_vma=False,
    )
```
